32 devices in a mesh: groups: 2 (over y), tiles: 4 (over z), sub: 2 (over x), modes: 2 (over core).
Axes of the slice: x: 2, y: 2, z: 4, core: 2. Of those that a mesh axis runs over, the one named last changes fastest.
Arguments:
- object_field: float32 [2, 2048, 1024], P(None, ('groups', 'tiles')), parts along dimension 1, may hold values from -5 to 5
- probe: bfloat16 [4, 256, 512], P('groups'), parts along dimension 0, may hold values from -6 to 6
- intensity: bfloat16 [8, 32, 256, 256], P(('groups', 'tiles'), ('sub', 'modes')), parts along dimension 0, may hold values from 0.099609375 to 10
- centres: int32 [8, 32, 2], P(('groups', 'tiles')), parts along dimension 0, may hold values from 128 to 896, as said below
- counts: int32 [8], P(('groups', 'tiles')), parts along dimension 0, may hold values from 1 to 32, 64 in all
Outputs:
- object_grad: float32 [2, 2048, 1024], P(None, ('groups', 'tiles'), ('sub', 'modes')), parts along dimension 1
- probe_grad: float32 [4, 256, 512], P('groups'), parts along dimension 0
The draws below stay inside these ranges and needn't reach their ends.
There are 2 independent parts, one for each index of `groups`. The reference program is written for one: setup_inputs(seed, part) draws one part's arguments, and reference() takes and returns one part's arrays. A program takes and returns all parts, laid end to end along the dimension named above; each array names one. Nothing has to cross between parts.
Inputs may be any that keep to these rules, and one draw needn't show every extreme that they name: centres[t, j, 0] is a row in [t * 256, (t + 1) * 256) and in [128, 896]; centres[t, j, 1] is a column in [128, 896]. Slots j >= counts[t] of strip t are not scan points and contribute nothing.
All inputs are finite; a program needn't handle non-finite values. No bound on the sum of `counts` on one device may be relied on, other than what follows from the above.
Results may differ from the reference program's by a relative error of at most 0.0041.
Values sent between devices are 32-bit elements; how exact they have to be, the bound alone decides.
No kernel may reach another device: no remote copies, remote signals or barrier semaphores. Data moves between devices by JAX's collectives and lax.ppermute only.
A program may use at most 64 MiB of HBM per device.

```python
import math
import jax
import jax.numpy as jnp
import numpy as np
from jax import lax

PATCH = 256
PROBE_MODES = 2
TR = 256
NC = 1024
PTS_STRIP = 32
NR = 1024
N_TILES = 4


def draw_centres(key, part):
    key = jax.random.fold_in(key, 11)
    row_key, col_key = jax.random.split(key)
    base = (jnp.arange(N_TILES, dtype=jnp.int32) * TR)[:, None]
    rows = base + jax.random.randint(row_key, (N_TILES, PTS_STRIP), 0, TR, dtype=jnp.int32)
    rows = jnp.clip(rows, PATCH // 2, TR * N_TILES - PATCH // 2)
    cols = jax.random.randint(col_key, (N_TILES, PTS_STRIP), PATCH // 2, NC - PATCH // 2 + 1, dtype=jnp.int32)
    return jnp.stack([rows, cols], axis=-1).astype(jnp.int32)


def levels(rng, dims, cuts, smallest, top_value):
    gain = 1.0
    for dim, parts in cuts:
        heights = jax.random.uniform(jax.random.fold_in(jax.random.fold_in(rng, 6), dim), (parts,), jnp.float32, smallest / len(cuts), top_value / len(cuts))
        gain = gain * jnp.repeat(jnp.exp(heights), dims[dim] // parts).reshape((-1,) + (1,) * (len(dims) - 1 - dim))
    return gain


def profile(count, total, most, skew):
    loads = [(1 << 20) // math.isqrt(standing ** skew) + 1 for standing in range(2, count + 1)]
    spare, given = total - most - (count - 1), [1] * (count - 1)
    while spare > 0:
        movable = [i for i in range(count - 1) if given[i] < most]
        mass, remaining = sum([loads[i] for i in movable]), spare
        for i in movable:
            extra = min(most - given[i], max(1, remaining * loads[i] // mass), spare)
            given[i] = given[i] + extra
            spare = spare - extra
    return np.array([most] + given)


def uneven(rng, amount, total, most, skew):
    if amount == 2:
        one = jax.random.randint(rng, (), max(1, total - most), min(most, total - 1) + 1)
        return jnp.stack([one, total - one])
    lengths = jnp.asarray(profile(amount, total, most, skew), jnp.int32)
    twos = (amount - 1) // 2
    donor, receiver = lengths[1:1 + 2 * twos:2], lengths[2:2 + 2 * twos:2]
    margin = jnp.minimum(donor - 1, most - receiver)
    shifted = jax.random.randint(jax.random.fold_in(rng, 1), (twos,), 0, 1 << 20) % (margin + 1)
    lengths = lengths.at[1:1 + 2 * twos:2].set(donor - shifted).at[2:2 + 2 * twos:2].set(receiver + shifted)
    return lengths[jax.random.permutation(jax.random.fold_in(rng, 2), amount)]


def scatter_about(key, shape, deviation, most, shards=(), kind=jnp.bfloat16):
    factor_of = levels(key, shape, shards, -0.22, 0.18) if shards else 1.0
    values = jax.random.normal(key, shape, jnp.float32) * deviation * factor_of
    return jnp.minimum(jnp.maximum(values, -most), most).astype(kind)


def setup_inputs(seed: int = 0, part: int = 0) -> dict:
    arg_keys = jax.random.split(jax.random.key(seed), 6)
    own_keys = jax.random.split(jax.random.fold_in(arg_keys[5], part), 6)
    return {
        "object_field": scatter_about(own_keys[0], (2, NR, NC), 0.7, 5.0, ((1, 4),), jnp.float32),
        "probe": scatter_about(own_keys[1], (PROBE_MODES, PATCH, 2 * PATCH), 1.0, 6.0),
        "intensity": jnp.clip(jnp.exp(math.log(10.0) - 4.609084 * jax.random.uniform(own_keys[2], (N_TILES, PTS_STRIP, PATCH, PATCH), jnp.float32) ** levels(own_keys[2], (N_TILES, PTS_STRIP, PATCH, PATCH), ((0, 4), (1, 4)), -0.2, 0.2)), 0.099609375, 10.0).astype(jnp.bfloat16),
        "centres": draw_centres(jax.random.fold_in(jax.random.fold_in(arg_keys[5], part), 71), part),
        "counts": uneven(own_keys[4], N_TILES, PTS_STRIP * N_TILES // 2, PTS_STRIP, 2).astype(jnp.int32),
    }


def dft_tables(size):
    index = jnp.arange(size, dtype=jnp.int32)
    wrapped = index[:, None] * index[None, :] % size
    angle = wrapped.astype(jnp.float32) * (2.0 * math.pi / size)
    scale = 1.0 / math.sqrt(size)
    return ((jnp.cos(angle) * scale).astype(jnp.bfloat16), (-jnp.sin(angle) * scale).astype(jnp.bfloat16))

def transform(field, cos_part, sin_part):
    size = cos_part.shape[0]
    left = jnp.concatenate([cos_part, sin_part], axis=0).astype(jnp.float32)
    right = jnp.concatenate([jnp.concatenate([cos_part, sin_part], axis=1), jnp.concatenate([-sin_part, cos_part], axis=1)], axis=0).astype(jnp.float32)
    stacked = jnp.einsum('ak,smkc->smac', left, field.astype(jnp.float32))
    real = stacked[..., :size, :size] - stacked[..., size:, size:]
    imag = stacked[..., :size, size:] + stacked[..., size:, :size]
    middle = jnp.concatenate([real, imag], axis=-1).astype(jnp.bfloat16)
    return jnp.einsum('smac,cd->smad', middle.astype(jnp.float32), right)

def point_terms(patches, probe, inten, cos_part, sin_part):
    size = probe.shape[1]
    probe_re = probe[None, :, :, :size].astype(jnp.float32)
    probe_im = probe[None, :, :, size:].astype(jnp.float32)
    obj_re = patches[:, None, :, :size]
    obj_im = patches[:, None, :, size:]
    wave = jnp.concatenate([probe_re * obj_re - probe_im * obj_im, probe_re * obj_im + probe_im * obj_re], axis=-1).astype(jnp.bfloat16)
    far = transform(wave, cos_part, sin_part)
    power = lax.optimization_barrier(jnp.sum(far[..., :size] ** 2 + far[..., size:] ** 2, axis=1))
    model = jnp.sqrt(power + 1.0)
    measured = jnp.sqrt(inten.astype(jnp.float32) + 1.0)
    ratio = 1.0 - measured / model
    chi = (far * jnp.concatenate([ratio, ratio], axis=-1)[:, None]).astype(jnp.bfloat16)
    back = transform(chi, cos_part, -sin_part)
    back_re = back[..., :size]
    back_im = back[..., size:]
    obj_terms = jnp.concatenate([lax.optimization_barrier(jnp.sum(probe_re * back_re + probe_im * back_im, axis=1)), lax.optimization_barrier(jnp.sum(probe_re * back_im - probe_im * back_re, axis=1))], axis=-1)
    probe_terms = jnp.concatenate([obj_re * back_re + obj_im * back_im, obj_re * back_im - obj_im * back_re], axis=-1)
    return (obj_terms, probe_terms)

def reference(object_field, probe, intensity, centres, counts):
    half = PATCH // 2
    cos_part, sin_part = dft_tables(PATCH)
    padded = jnp.pad(object_field, ((0, 0), (half, half), (0, 0)))
    slots = jnp.arange(PTS_STRIP, dtype=jnp.int32)

    def strip(carry, inputs):
        grad, probe_total = carry
        inten, spots, count = inputs
        valid = (slots < count).astype(jnp.float32)

        def cut(spot):
            piece = lax.dynamic_slice(padded, (jnp.int32(0), spot[0], spot[1] - half), (2, PATCH, PATCH))
            return jnp.concatenate([piece[0], piece[1]], axis=-1)
        patches = jax.vmap(cut)(spots)
        obj_terms, probe_terms = point_terms(patches, probe, inten, cos_part, sin_part)
        probe_total = probe_total + lax.optimization_barrier(jnp.sum(probe_terms * valid[:, None, None, None], axis=0))

        def place(slot, grad):
            spot = spots[slot]
            update = obj_terms[slot] * valid[slot]
            update = jnp.stack([update[:, :PATCH], update[:, PATCH:]])
            start = (jnp.int32(0), spot[0], spot[1] - half)
            return lax.dynamic_update_slice(grad, lax.dynamic_slice(grad, start, (2, PATCH, PATCH)) + update, start)
        grad = lax.fori_loop(0, PTS_STRIP, place, grad)
        return ((grad, probe_total), None)
    init = (jnp.zeros(padded.shape, jnp.float32), jnp.zeros((PROBE_MODES, PATCH, 2 * PATCH), jnp.float32))
    (grad, probe_total), unused = lax.scan(strip, init, (intensity, centres, counts))
    return (grad[:, half:half + TR * N_TILES], probe_total)
```

```python
import functools
import math

import jax
import jax.numpy as jnp
import ml_dtypes
import numpy as np
from jax import lax
from jax.experimental import pallas as pl
from jax.experimental.pallas import tpu as pltpu
from jax.sharding import PartitionSpec as P

LANES = 128
CHUNK = 64


def dft_tables(size):
    index = np.arange(size)
    angle = (index[:, None] * index[None, :] % size) * (2.0 * math.pi / size)
    scale = 1.0 / math.sqrt(size)
    cos_part = (np.cos(angle) * scale).astype(np.float32).astype(ml_dtypes.bfloat16)
    sin_part = (-np.sin(angle) * scale).astype(np.float32).astype(ml_dtypes.bfloat16)
    plain = np.block([[cos_part, -sin_part], [sin_part, cos_part]])
    turned = np.block([[cos_part, sin_part], [-sin_part, cos_part]])
    return plain, turned


def point_kernel(
    place,
    counts,
    spots,
    own,
    up_a,
    dn_a,
    up_b,
    dn_b,
    probe,
    inten,
    plain,
    turned,
    *rest,
    owners,
):
    outs = rest[:owners]
    probe_grad = rest[owners]
    field, grad, probe_f32, patch, wave, half_buf, far, sems, out_sems = rest[owners + 1 :]
    strip, sub, mode = place[0], place[1], place[2]
    member = sub * 2 + mode
    side = probe.shape[1]
    rim = side // 2
    strip_rows = own.shape[1]
    blocks = own.shape[2] // LANES
    slots = inten.shape[0]
    total = jnp.clip(counts[0] - member * slots, 0, slots)

    copies = []

    def fetch(src, dst):
        copies.append(pltpu.make_async_copy(src, dst, sems.at[len(copies)]))

    for block in range(blocks):
        cols = pl.ds(block * LANES, LANES)
        for plane in range(2):
            fetch(own.at[plane, :, cols], field.at[plane, block, pl.ds(rim, strip_rows)])
        for up, dn, plane in ((up_a, dn_a, mode), (up_b, dn_b, 1 - mode)):
            fetch(up.at[:, cols], field.at[plane, block, pl.ds(0, rim)])
            fetch(dn.at[:, cols], field.at[plane, block, pl.ds(rim + strip_rows, rim)])
    for copy in copies:
        copy.start()

    probe_grad[...] = jnp.zeros_like(probe_grad)
    for m in range(2):
        probe_f32[m] = probe[m].astype(jnp.float32)

    @pl.loop(0, grad.shape[0])
    def clear(block):
        grad[block] = jnp.zeros(grad.shape[1:], jnp.float32)

    for copy in copies:
        copy.wait()

    lane = lax.broadcasted_iota(jnp.int32, (CHUNK, LANES), 1)

    @pl.loop(0, total)
    def point(slot):
        base = 2 * (member * slots + slot)
        row = spots[base] - strip * strip_rows
        col = spots[base + 1] - rim
        block = col // LANES
        off = col % LANES
        back_shift = (LANES - off) % LANES
        for plane in range(2):
            for chunk in range(0, side, CHUNK):
                rows = pl.ds(row + chunk, CHUNK)
                rolled = [
                    pltpu.roll(field[plane, block + j, rows, :], back_shift, 1) for j in range(3)
                ]
                for j in range(2):
                    patch[plane, chunk : chunk + CHUNK, j * LANES : (j + 1) * LANES] = jnp.where(
                        lane < LANES - off, rolled[j], rolled[j + 1]
                    )
        for chunk in range(0, side, CHUNK):
            rows = slice(chunk, chunk + CHUNK)
            obj_re, obj_im = patch[0, rows], patch[1, rows]
            for m in range(2):
                probe_re = probe_f32[m, rows, :side]
                probe_im = probe_f32[m, rows, side:]
                cols = slice(m * side, (m + 1) * side)
                wave[rows, cols] = (probe_re * obj_re - probe_im * obj_im).astype(jnp.bfloat16)
                wave[side + chunk : side + chunk + CHUNK, cols] = (
                    probe_re * obj_im + probe_im * obj_re
                ).astype(jnp.bfloat16)
        for m in range(2):
            cols = slice(m * side, (m + 1) * side)
            stacked = jnp.dot(plain[...], wave[:, cols], preferred_element_type=jnp.float32)
            half_buf[cols, :side] = stacked[:side].astype(jnp.bfloat16)
            half_buf[cols, side:] = stacked[side:].astype(jnp.bfloat16)
        for m in range(2):
            rows = slice(m * side, (m + 1) * side)
            far[rows] = jnp.dot(half_buf[rows], turned[...], preferred_element_type=jnp.float32)
        for chunk in range(0, side, CHUNK):
            parts = []
            power = 1.0
            for m in range(2):
                rows = slice(m * side + chunk, m * side + chunk + CHUNK)
                far_re, far_im = far[rows, :side], far[rows, side:]
                power = power + (far_re * far_re + far_im * far_im)
                parts.append((far_re, far_im))
            level = inten[slot, chunk : chunk + CHUNK].astype(jnp.float32) + 1.0
            ratio = 1.0 - level * lax.rsqrt(level * power)
            for m in range(2):
                cols = slice(m * side, (m + 1) * side)
                wave[chunk : chunk + CHUNK, cols] = (parts[m][0] * ratio).astype(jnp.bfloat16)
                wave[side + chunk : side + chunk + CHUNK, cols] = (parts[m][1] * ratio).astype(
                    jnp.bfloat16
                )
        for m in range(2):
            cols = slice(m * side, (m + 1) * side)
            stacked = jnp.dot(turned[...], wave[:, cols], preferred_element_type=jnp.float32)
            half_buf[cols, :side] = stacked[:side].astype(jnp.bfloat16)
            half_buf[cols, side:] = stacked[side:].astype(jnp.bfloat16)
        for m in range(2):
            rows = slice(m * side, (m + 1) * side)
            far[rows] = jnp.dot(half_buf[rows], plain[...], preferred_element_type=jnp.float32)
        for chunk in range(0, side, CHUNK):
            rows = slice(chunk, chunk + CHUNK)
            obj_re, obj_im = patch[0, rows], patch[1, rows]
            terms = [0.0, 0.0]
            for m in range(2):
                probe_re = probe_f32[m, rows, :side]
                probe_im = probe_f32[m, rows, side:]
                far_rows = slice(m * side + chunk, m * side + chunk + CHUNK)
                back_re, back_im = far[far_rows, :side], far[far_rows, side:]
                terms[0] = terms[0] + (probe_re * back_re + probe_im * back_im)
                terms[1] = terms[1] + (probe_re * back_im - probe_im * back_re)
                probe_grad[m, rows, :side] += obj_re * back_re + obj_im * back_im
                probe_grad[m, rows, side:] += obj_re * back_im - obj_im * back_re
            target = pl.ds(row + chunk, CHUNK)
            for plane in range(2):
                left = pltpu.roll(terms[plane][:, :LANES], off, 1)
                right = pltpu.roll(terms[plane][:, LANES:], off, 1)
                grad[block, plane, target, :] += jnp.where(lane < off, 0.0, left)
                grad[block + 1, plane, target, :] += jnp.where(lane < off, left, right)
                grad[block + 2, plane, target, :] += jnp.where(lane < off, right, 0.0)

    width = blocks // owners
    sends = []
    for step in range(owners // 2):
        for swap in range(2):
            owner = 2 * lax.rem(sub + step, owners // 2) + (mode + swap) % 2
            index = 2 * step + swap
            sends.append(
                pltpu.make_async_copy(
                    grad.at[pl.ds(owner * width, width)], outs[index], out_sems.at[index]
                )
            )
    for copy in sends:
        copy.start()
    for copy in sends:
        copy.wait()


def point_sums(place, counts, spots, own, halos, probe, inten, owners):
    plain, turned = dft_tables(probe.shape[1])
    side = probe.shape[1]
    blocks = own.shape[2] // LANES
    rows = own.shape[1] + side
    piece = jax.ShapeDtypeStruct((blocks // owners, 2, rows, LANES), jnp.float32)
    smem = pl.BlockSpec(memory_space=pltpu.SMEM)
    vmem = pl.BlockSpec(memory_space=pltpu.VMEM)
    anywhere = pl.BlockSpec(memory_space=pl.ANY)
    slots = inten.shape[0]
    return pl.pallas_call(
        functools.partial(point_kernel, owners=owners),
        out_shape=[piece] * owners
        + [jax.ShapeDtypeStruct((2, side, 2 * side), jnp.float32)],
        in_specs=[smem] * 3 + [anywhere] * 5 + [vmem] * 4,
        out_specs=[anywhere] * owners + [vmem],
        scratch_shapes=[
            pltpu.VMEM((2, blocks + 1, rows, LANES), jnp.float32),
            pltpu.VMEM((blocks + 1, 2, rows, LANES), jnp.float32),
            pltpu.VMEM((2, side, 2 * side), jnp.float32),
            pltpu.VMEM((2, side, side), jnp.float32),
            pltpu.VMEM((2 * side, 2 * side), jnp.bfloat16),
            pltpu.VMEM((2 * side, 2 * side), jnp.bfloat16),
            pltpu.VMEM((2 * side, 2 * side), jnp.float32),
            pltpu.SemaphoreType.DMA((6 * blocks,)),
            pltpu.SemaphoreType.DMA((owners,)),
        ],
        compiler_params=pltpu.CompilerParams(vmem_limit_bytes=60 * 1024 * 1024),
        cost_estimate=pl.CostEstimate(
            flops=slots * 32 * 2 * side**3, bytes_accessed=16 * 1024 * 1024, transcendentals=0
        ),
        name="point_sums",
    )(place, counts, spots, own, *halos, probe, inten, jnp.asarray(plain), jnp.asarray(turned))


def shift_up(cells, axis):
    count = lax.axis_size(axis)
    return lax.ppermute(cells, axis, [(i, i + 1) for i in range(count - 1)])


def shift_down(cells, axis):
    count = lax.axis_size(axis)
    return lax.ppermute(cells, axis, [(i + 1, i) for i in range(count - 1)])


def rotated(cells, axis, step):
    count = lax.axis_size(axis)
    return lax.ppermute(cells, axis, [(i, (i + step) % count) for i in range(count)])


def scatter_sum(cells, axis):
    count = lax.axis_size(axis)
    share = cells.shape[0] // count
    index = lax.axis_index(axis)
    turned = lax.dynamic_slice_in_dim(
        jnp.concatenate([cells, cells]), index * share, cells.shape[0], 0
    )
    total = turned[:share]
    for step in range(1, count):
        total = total + rotated(turned[step * share : (step + 1) * share], axis, step)
    return total


def gather_parts(part, axis):
    count = lax.axis_size(axis)
    index = lax.axis_index(axis)
    parts = [part] + [rotated(part, axis, step) for step in range(1, count)]
    parts = jnp.concatenate(parts[:1] + parts[:0:-1])
    share = part.shape[0]
    start = (count - index) % count * share
    return lax.dynamic_slice_in_dim(jnp.concatenate([parts, parts]), start, count * share, 0)


def sum_over_strips(cells):
    if lax.axis_size("tiles") > 4:
        return lax.psum(cells, ("tiles", "sub"))
    middle = cells.shape[0] // 2
    first = scatter_sum(cells[:middle], "tiles")
    second = scatter_sum(cells[middle:], "sub")
    for step in range(1, lax.axis_size("sub")):
        first = first + rotated(first, "sub", step)
    second = scatter_sum(second, "tiles")
    second = gather_parts(second, "tiles")
    first = gather_parts(first, "tiles")
    second = gather_parts(second, "sub")
    return jnp.concatenate([first, second])


def swap(cells):
    return lax.ppermute(cells, "modes", [(0, 1), (1, 0)])


def on_device(object_field, probe, intensity, centres, counts):
    side = probe.shape[1]
    rim = side // 2
    strip_rows = object_field.shape[1]
    strip = lax.axis_index("tiles")
    sub = lax.axis_index("sub")
    mode = lax.axis_index("modes")
    subs = lax.axis_size("sub")
    owners = subs * lax.axis_size("modes")
    place = jnp.stack([strip, sub, mode]).astype(jnp.int32)

    own_plane = lax.dynamic_index_in_dim(object_field, mode, 0, keepdims=False)
    up_a = shift_up(own_plane[strip_rows - rim :], "tiles")
    dn_a = shift_down(own_plane[:rim], "tiles")
    halos = (up_a, dn_a, swap(up_a), swap(dn_a))

    sums = point_sums(
        place, counts, centres.reshape(-1), object_field, halos, probe, intensity[0], owners
    )
    probe_grad = sums[owners]

    mine = []
    for step in range(subs):
        mine.append(sums[2 * step] + swap(sums[2 * step + 1]))
    total = mine[0]
    for step in range(1, subs):
        total = total + lax.ppermute(
            mine[step], "sub", [(i, (i + step) % subs) for i in range(subs)]
        )
    total = total.transpose(1, 2, 0, 3).reshape(2, strip_rows + side, -1)
    core = total[:, rim : rim + strip_rows]
    core = core.at[:, :rim].add(shift_up(total[:, rim + strip_rows :], "tiles"))
    core = core.at[:, strip_rows - rim :].add(shift_down(total[:, :rim], "tiles"))

    kept = lax.dynamic_index_in_dim(probe_grad, mode, 0, keepdims=False)
    given = lax.dynamic_index_in_dim(probe_grad, 1 - mode, 0, keepdims=False)
    kept = sum_over_strips(kept + swap(given))
    other = swap(kept)
    probe_out = jnp.where(mode == 0, jnp.stack([kept, other]), jnp.stack([other, kept]))
    return (core, probe_out)


def solution(mesh):
    return jax.shard_map(
        on_device,
        mesh=mesh,
        in_specs=(
            P(None, ("groups", "tiles"), None),
            P("groups", None, None),
            P(("groups", "tiles"), ("sub", "modes"), None, None),
            P(("groups", "tiles"), None, None),
            P(("groups", "tiles")),
        ),
        out_specs=(P(None, ("groups", "tiles"), ("sub", "modes")), P("groups", None, None)),
        check_vma=False,
    )
```

```python
import functools
import math

import jax
import jax.numpy as jnp
import ml_dtypes
import numpy as np
from jax import lax
from jax.experimental import pallas as pl
from jax.experimental.pallas import tpu as pltpu
from jax.sharding import PartitionSpec as P

LANES = 128
CHUNK = 64


def dft_tables(size):
    index = np.arange(size)
    angle = (index[:, None] * index[None, :] % size) * (2.0 * math.pi / size)
    scale = 1.0 / math.sqrt(size)
    cos_part = (np.cos(angle) * scale).astype(np.float32).astype(ml_dtypes.bfloat16)
    sin_part = (-np.sin(angle) * scale).astype(np.float32).astype(ml_dtypes.bfloat16)
    plain = np.block([[cos_part, -sin_part], [sin_part, cos_part]])
    turned = np.block([[cos_part, sin_part], [-sin_part, cos_part]])
    return plain, turned


def point_kernel(
    place,
    counts,
    spots,
    own,
    up_a,
    dn_a,
    up_b,
    dn_b,
    probe,
    inten,
    plain,
    turned,
    *rest,
    owners,
):
    keep_obj, give_mine, give_others, keep_probe, give_probe = rest[:5]
    field, grad, probe_grad, probe_f32, patch, wave, half_buf, far, sems, out_sems = rest[5:]
    strip, sub, mode = place[0], place[1], place[2]
    member = sub * 2 + mode
    side = probe.shape[1]
    rim = side // 2
    strip_rows = own.shape[1]
    blocks = own.shape[2] // LANES
    slots = inten.shape[0]
    total = jnp.clip(counts[0] - member * slots, 0, slots)

    copies = []

    def fetch(src, dst):
        copies.append(pltpu.make_async_copy(src, dst, sems.at[len(copies)]))

    for block in range(blocks):
        cols = pl.ds(block * LANES, LANES)
        for plane in range(2):
            fetch(own.at[plane, :, cols], field.at[plane, block, pl.ds(rim, strip_rows)])
        for up, dn, plane in ((up_a, dn_a, mode), (up_b, dn_b, 1 - mode)):
            fetch(up.at[:, cols], field.at[plane, block, pl.ds(0, rim)])
            fetch(dn.at[:, cols], field.at[plane, block, pl.ds(rim + strip_rows, rim)])
    for copy in copies:
        copy.start()

    probe_grad[...] = jnp.zeros_like(probe_grad)
    for m in range(2):
        probe_f32[m] = probe[m].astype(jnp.float32)

    @pl.loop(0, grad.shape[0])
    def clear(block):
        grad[block] = jnp.zeros(grad.shape[1:], jnp.float32)

    for copy in copies:
        copy.wait()

    lane = lax.broadcasted_iota(jnp.int32, (CHUNK, LANES), 1)

    @pl.loop(0, total)
    def point(slot):
        base = 2 * (member * slots + slot)
        row = spots[base] - strip * strip_rows
        col = spots[base + 1] - rim
        block = col // LANES
        off = col % LANES
        back_shift = (LANES - off) % LANES
        for plane in range(2):
            for chunk in range(0, side, CHUNK):
                rows = pl.ds(row + chunk, CHUNK)
                rolled = [
                    pltpu.roll(field[plane, block + j, rows, :], back_shift, 1) for j in range(3)
                ]
                for j in range(2):
                    patch[plane, chunk : chunk + CHUNK, j * LANES : (j + 1) * LANES] = jnp.where(
                        lane < LANES - off, rolled[j], rolled[j + 1]
                    )
        for chunk in range(0, side, CHUNK):
            rows = slice(chunk, chunk + CHUNK)
            obj_re, obj_im = patch[0, rows], patch[1, rows]
            for m in range(2):
                probe_re = probe_f32[m, rows, :side]
                probe_im = probe_f32[m, rows, side:]
                cols = slice(m * side, (m + 1) * side)
                wave[rows, cols] = (probe_re * obj_re - probe_im * obj_im).astype(jnp.bfloat16)
                wave[side + chunk : side + chunk + CHUNK, cols] = (
                    probe_re * obj_im + probe_im * obj_re
                ).astype(jnp.bfloat16)
        for m in range(2):
            cols = slice(m * side, (m + 1) * side)
            stacked = jnp.dot(plain[...], wave[:, cols], preferred_element_type=jnp.float32)
            half_buf[cols, :side] = stacked[:side].astype(jnp.bfloat16)
            half_buf[cols, side:] = stacked[side:].astype(jnp.bfloat16)
        for m in range(2):
            rows = slice(m * side, (m + 1) * side)
            far[rows] = jnp.dot(half_buf[rows], turned[...], preferred_element_type=jnp.float32)
        for chunk in range(0, side, CHUNK):
            parts = []
            power = 1.0
            for m in range(2):
                rows = slice(m * side + chunk, m * side + chunk + CHUNK)
                far_re, far_im = far[rows, :side], far[rows, side:]
                power = power + (far_re * far_re + far_im * far_im)
                parts.append((far_re, far_im))
            level = inten[slot, chunk : chunk + CHUNK].astype(jnp.float32) + 1.0
            ratio = 1.0 - level * lax.rsqrt(level * power)
            for m in range(2):
                cols = slice(m * side, (m + 1) * side)
                wave[chunk : chunk + CHUNK, cols] = (parts[m][0] * ratio).astype(jnp.bfloat16)
                wave[side + chunk : side + chunk + CHUNK, cols] = (parts[m][1] * ratio).astype(
                    jnp.bfloat16
                )
        for m in range(2):
            cols = slice(m * side, (m + 1) * side)
            stacked = jnp.dot(turned[...], wave[:, cols], preferred_element_type=jnp.float32)
            half_buf[cols, :side] = stacked[:side].astype(jnp.bfloat16)
            half_buf[cols, side:] = stacked[side:].astype(jnp.bfloat16)
        for m in range(2):
            rows = slice(m * side, (m + 1) * side)
            far[rows] = jnp.dot(half_buf[rows], plain[...], preferred_element_type=jnp.float32)
        for chunk in range(0, side, CHUNK):
            rows = slice(chunk, chunk + CHUNK)
            obj_re, obj_im = patch[0, rows], patch[1, rows]
            terms = [0.0, 0.0]
            for m in range(2):
                probe_re = probe_f32[m, rows, :side]
                probe_im = probe_f32[m, rows, side:]
                far_rows = slice(m * side + chunk, m * side + chunk + CHUNK)
                back_re, back_im = far[far_rows, :side], far[far_rows, side:]
                terms[0] = terms[0] + (probe_re * back_re + probe_im * back_im)
                terms[1] = terms[1] + (probe_re * back_im - probe_im * back_re)
                probe_grad[m, rows, :side] += obj_re * back_re + obj_im * back_im
                probe_grad[m, rows, side:] += obj_re * back_im - obj_im * back_re
            target = pl.ds(row + chunk, CHUNK)
            for plane in range(2):
                left = pltpu.roll(terms[plane][:, :LANES], off, 1)
                right = pltpu.roll(terms[plane][:, LANES:], off, 1)
                grad[block, plane, target, :] += jnp.where(lane < off, 0.0, left)
                grad[block + 1, plane, target, :] += jnp.where(lane < off, left, right)
                grad[block + 2, plane, target, :] += jnp.where(lane < off, right, 0.0)

    width = blocks // owners
    sends = []

    def send(src, dst):
        sends.append(pltpu.make_async_copy(src, dst, out_sems.at[len(sends)]))

    send(probe_grad.at[1 - mode], give_probe)
    send(probe_grad.at[mode], keep_probe)
    for step in list(range(1, owners // 2)) + [0]:
        owner = 2 * lax.rem(sub + step, owners // 2)
        target = give_others.at[pl.ds((step - 1) * width, width)] if step else give_mine
        send(grad.at[pl.ds((owner + 1 - mode) * width, width)], target)
        send(
            grad.at[pl.ds((owner + mode) * width, width)],
            keep_obj.at[pl.ds(step * width, width)],
        )
    for copy in sends:
        copy.start()
    for copy in sends:
        copy.wait()


def point_sums(place, counts, spots, own, halos, probe, inten, owners):
    plain, turned = dft_tables(probe.shape[1])
    side = probe.shape[1]
    blocks = own.shape[2] // LANES
    rows = own.shape[1] + side
    width = blocks // owners

    def piece(count):
        return jax.ShapeDtypeStruct((count, 2, rows, LANES), jnp.float32)

    mode_sum = jax.ShapeDtypeStruct((side, 2 * side), jnp.float32)
    smem = pl.BlockSpec(memory_space=pltpu.SMEM)
    vmem = pl.BlockSpec(memory_space=pltpu.VMEM)
    anywhere = pl.BlockSpec(memory_space=pl.ANY)
    slots = inten.shape[0]
    return pl.pallas_call(
        functools.partial(point_kernel, owners=owners),
        out_shape=[piece(blocks // 2), piece(width), piece(blocks // 2 - width), mode_sum, mode_sum],
        in_specs=[smem] * 3 + [anywhere] * 5 + [vmem] * 4,
        out_specs=[anywhere] * 5,
        scratch_shapes=[
            pltpu.VMEM((2, blocks + 1, rows, LANES), jnp.float32),
            pltpu.VMEM((blocks + 1, 2, rows, LANES), jnp.float32),
            pltpu.VMEM((2, side, 2 * side), jnp.float32),
            pltpu.VMEM((2, side, 2 * side), jnp.float32),
            pltpu.VMEM((2, side, side), jnp.float32),
            pltpu.VMEM((2 * side, 2 * side), jnp.bfloat16),
            pltpu.VMEM((2 * side, 2 * side), jnp.bfloat16),
            pltpu.VMEM((2 * side, 2 * side), jnp.float32),
            pltpu.SemaphoreType.DMA((6 * blocks,)),
            pltpu.SemaphoreType.DMA((owners + 2,)),
        ],
        compiler_params=pltpu.CompilerParams(vmem_limit_bytes=60 * 1024 * 1024),
        cost_estimate=pl.CostEstimate(
            flops=slots * 32 * 2 * side**3, bytes_accessed=16 * 1024 * 1024, transcendentals=0
        ),
        name="point_sums",
    )(place, counts, spots, own, *halos, probe, inten, jnp.asarray(plain), jnp.asarray(turned))


def shift_up(cells, axis):
    count = lax.axis_size(axis)
    return lax.ppermute(cells, axis, [(i, i + 1) for i in range(count - 1)])


def shift_down(cells, axis):
    count = lax.axis_size(axis)
    return lax.ppermute(cells, axis, [(i + 1, i) for i in range(count - 1)])


def swap(cells):
    return lax.ppermute(cells, "modes", [(0, 1), (1, 0)])


def rotated(cells, axis, step):
    count = lax.axis_size(axis)
    return lax.ppermute(cells, axis, [(i, (i + step) % count) for i in range(count)])


def small_kernel(body, out_shape, *args, name):
    return pl.pallas_call(
        body,
        out_shape=out_shape,
        in_specs=[
            pl.BlockSpec(memory_space=pltpu.SMEM if x.dtype == jnp.int32 else pltpu.VMEM)
            for x in args
        ],
        out_specs=jax.tree.map(lambda _: pl.BlockSpec(memory_space=pltpu.VMEM), out_shape),
        compiler_params=pltpu.CompilerParams(vmem_limit_bytes=24 * 1024 * 1024),
        cost_estimate=pl.CostEstimate(flops=0, bytes_accessed=0, transcendentals=0),
        name=name,
    )(*args)


def shape(*dims):
    return jax.ShapeDtypeStruct(dims, jnp.float32)


def after(cells, *earlier):
    return lax.optimization_barrier((cells, *earlier))[0]


def add_kernel(*refs):
    total = refs[0][...]
    for ref in refs[1:-1]:
        total = total + ref[...]
    refs[-1][...] = total


def others_kernel(kept, got, *outs):
    width, _, rows = outs[1].shape[:3]
    rim = outs[0].shape[2] // 2
    for step in range(len(outs) // 2):
        rims, core = outs[2 * step : 2 * step + 2]
        mine = slice((step + 1) * width, (step + 2) * width)
        theirs = slice(step * width, (step + 1) * width)
        rims[:, :, :rim] = kept[mine, :, :rim] + got[theirs, :, :rim]
        rims[:, :, rim:] = kept[mine, :, rim + rows :] + got[theirs, :, rim + rows :]
        core[...] = kept[mine, :, rim : rim + rows] + got[theirs, :, rim : rim + rows]


def mine_kernel(kept, got, *rest):
    above, core, below = rest[-3:]
    width = got.shape[0]
    rim, rows = above.shape[2], core.shape[2]
    total_above = kept[:width, :, :rim] + got[:, :, :rim]
    total_below = kept[:width, :, rim + rows :] + got[:, :, rim + rows :]
    for other in rest[:-3]:
        total_above = total_above + other[:, :, :rim]
        total_below = total_below + other[:, :, rim:]
    above[...] = total_above
    below[...] = total_below
    core[...] = kept[:width, :, rim : rim + rows] + got[:, :, rim : rim + rows]


def fold_kernel(core, from_below, from_above, out):
    rim, rows = from_below.shape[2], core.shape[2]
    out[...] = core[...]
    out[:, :, :rim] += from_above[...]
    out[:, :, rows - rim :] += from_below[...]


def finish_kernel(core, *rest):
    out = rest[-1]
    for block in range(core.shape[0]):
        total = core[block]
        for other in rest[:-1]:
            total = total + other[block]
        out[:, :, block * LANES : (block + 1) * LANES] = total


def share_rows(index, share):
    return pl.ds(pl.multiple_of(index * share, share), share)


def shares_kernel(place, kept, got, *outs):
    share = outs[0].shape[0]
    for step, out in enumerate(outs):
        rows = share_rows(lax.rem(place[0] + step, len(outs)), share)
        out[...] = kept[rows] + got[rows]


def order_kernel(place, *refs):
    out = refs[-1]
    share = refs[0].shape[0]
    tiles = len(refs) - 1
    for step, part in enumerate(refs[:-1]):
        out[share_rows(lax.rem(place[0] + tiles - step, tiles), share)] = part[...]


def both_kernel(place, mine, other, out):
    out[place[2]] = mine[...]
    out[1 - place[2]] = other[...]


def on_device(object_field, probe, intensity, centres, counts):
    side = probe.shape[1]
    rim = side // 2
    strip_rows, cols = object_field.shape[1:]
    strip = lax.axis_index("tiles")
    sub = lax.axis_index("sub")
    mode = lax.axis_index("modes")
    tiles, subs = lax.axis_size("tiles"), lax.axis_size("sub")
    owners = subs * lax.axis_size("modes")
    width = cols // owners // LANES
    place = jnp.stack([strip, sub, mode]).astype(jnp.int32)

    own_plane = lax.dynamic_index_in_dim(object_field, mode, 0, keepdims=False)
    up_a = shift_up(own_plane[strip_rows - rim :], "tiles")
    dn_a = shift_down(own_plane[:rim], "tiles")
    halos = (up_a, dn_a, swap(up_a), swap(dn_a))

    keep_obj, give_mine, give_others, keep_probe, give_probe = point_sums(
        place, counts, centres.reshape(-1), object_field, halos, probe, intensity[0], owners
    )
    got_probe = swap(give_probe)
    got_others = swap(give_others)
    got_mine = swap(give_mine)

    rims_shape = shape(width, 2, 2 * rim, LANES)
    core_shape = shape(width, 2, strip_rows, LANES)
    outgoing = list(small_kernel(
        others_kernel,
        [rims_shape, core_shape] * (subs - 1),
        keep_obj,
        got_others,
        name="object_others",
    ))

    def rotate_all(parts):
        return [rotated(x, "sub", step + 1) for step, x in enumerate(parts)]

    def rotate_strips(parts):
        return [rotated(x, "tiles", step + 1) for step, x in enumerate(parts)]

    direct = tiles <= 4
    total_rows, total_cols = keep_probe.shape
    share = shape(total_rows // tiles, total_cols)
    if direct:
        parts = small_kernel(
            shares_kernel, [share] * tiles, place, keep_probe, got_probe, name="probe_shares"
        )
        parts_in = rotate_strips(parts[1:])
    rims_in = rotate_all(outgoing[0::2])
    core_out = outgoing[1::2]
    above, core, below = small_kernel(
        mine_kernel,
        [shape(width, 2, rim, LANES), core_shape, shape(width, 2, rim, LANES)],
        keep_obj,
        got_mine,
        *rims_in,
        name="object_mine",
    )
    if direct:
        part_sum = small_kernel(add_kernel, share, parts[0], *parts_in, name="probe_strips_sum")
        part_sum, above, below = lax.optimization_barrier((part_sum, above, below))
        part_in = [rotated(part_sum, "sub", step) for step in range(1, subs)]
    from_below = shift_down(above, "tiles")
    from_above = shift_up(below, "tiles")
    folded = small_kernel(
        fold_kernel, core_shape, core, from_below, from_above, name="object_fold"
    )
    if direct:
        part_sum = small_kernel(add_kernel, share, part_sum, *part_in, name="probe_total")
        part_sum, folded, *core_out = lax.optimization_barrier((part_sum, folded, *core_out))
        parts_in = rotate_strips([part_sum] * (tiles - 1))
    core_in = rotate_all(core_out)
    if direct:
        probe_mine = small_kernel(
            order_kernel,
            shape(total_rows, total_cols),
            place,
            part_sum,
            *parts_in,
            name="probe_order",
        )
    else:
        probe_mine = lax.psum(keep_probe + got_probe, ("tiles", "sub"))
    object_grad = small_kernel(
        finish_kernel,
        shape(2, strip_rows, width * LANES),
        folded,
        *core_in,
        name="object_finish",
    )
    probe_grad = small_kernel(
        both_kernel,
        shape(2, *probe_mine.shape),
        place,
        probe_mine,
        swap(probe_mine),
        name="probe_both",
    )
    return (object_grad, probe_grad)


def solution(mesh):
    return jax.shard_map(
        on_device,
        mesh=mesh,
        in_specs=(
            P(None, ("groups", "tiles"), None),
            P("groups", None, None),
            P(("groups", "tiles"), ("sub", "modes"), None, None),
            P(("groups", "tiles"), None, None),
            P(("groups", "tiles")),
        ),
        out_specs=(P(None, ("groups", "tiles"), ("sub", "modes")), P("groups", None, None)),
        check_vma=False,
    )
```

```python
import functools
import math

import jax
import jax.numpy as jnp
import ml_dtypes
import numpy as np
from jax import lax
from jax.experimental import pallas as pl
from jax.experimental.pallas import tpu as pltpu
from jax.sharding import PartitionSpec as P

LANES = 128
CHUNK = 64


def dft_tables(size):
    index = np.arange(size)
    angle = (index[:, None] * index[None, :] % size) * (2.0 * math.pi / size)
    scale = 1.0 / math.sqrt(size)
    cos_part = (np.cos(angle) * scale).astype(np.float32).astype(ml_dtypes.bfloat16)
    sin_part = (-np.sin(angle) * scale).astype(np.float32).astype(ml_dtypes.bfloat16)
    plain = np.block([[cos_part, -sin_part], [sin_part, cos_part]])
    turned = np.block([[cos_part, sin_part], [-sin_part, cos_part]])
    return plain, turned


def interleave(first, second):
    done = 0
    for index, step in enumerate(first):
        step()
        upto = (index + 1) * len(second) // len(first)
        for other in second[done:upto]:
            other()
        done = upto


def point_kernel(
    place,
    counts,
    spots,
    own,
    first_a,
    second_a,
    first_b,
    second_b,
    probe_f32,
    inten,
    plain,
    turned,
    *rest,
    owners,
):
    keep_mine, give_mine, keep_others, give_others, keep_probe, give_probe = rest[:6]
    field, grad, probe_grad = rest[6:9]
    patches, waves, halves, fars = (rest[9 + 2 * i : 11 + 2 * i] for i in range(4))
    sems, out_sems = rest[17:]
    strip, sub, mode = place[0], place[1], place[2]
    member = sub * 2 + mode
    side = probe_f32.shape[1]
    rim = side // 2
    strip_rows = own.shape[1]
    blocks = own.shape[2] // LANES
    slots = inten.shape[0]
    total = jnp.clip(counts[0] - member * slots, 0, slots)
    far_rows = rim + strip_rows
    near = (strip % 2) * far_rows
    copies = []

    def fetch(src, dst):
        copies.append(pltpu.make_async_copy(src, dst, sems.at[len(copies)]))

    for block in range(blocks):
        cols = pl.ds(block * LANES, LANES)
        for plane in range(2):
            fetch(own.at[plane, :, cols], field.at[plane, block, pl.ds(rim, strip_rows)])
        for first, second, plane in ((first_a, second_a, mode), (first_b, second_b, 1 - mode)):
            fetch(first.at[:, cols], field.at[plane, block, pl.ds(far_rows - near, rim)])
            fetch(second.at[:, cols], field.at[plane, block, pl.ds(near, rim)])
    for copy in copies:
        copy.start()

    probe_grad[...] = jnp.zeros_like(probe_grad)
    patches[1][...] = jnp.zeros_like(patches[1])
    fars[1][...] = jnp.zeros_like(fars[1])

    @pl.loop(0, grad.shape[0])
    def clear(block):
        grad[block] = jnp.zeros(grad.shape[1:], jnp.float32)

    for copy in copies:
        copy.wait()

    lane = lax.broadcasted_iota(jnp.int32, (CHUNK, LANES), 1)
    chunks = range(0, side, CHUNK)

    def spot(slot):
        base = 2 * (member * slots + jnp.clip(slot, 0, slots - 1))
        row = spots[base] - strip * strip_rows
        col = spots[base + 1] - rim
        return row, col // LANES, col % LANES

    def cut(k, slot):
        row, block, off = spot(slot)
        back_shift = (LANES - off) % LANES
        patch, wave = patches[k], waves[k]

        def step(chunk):
            rows = slice(chunk, chunk + CHUNK)
            low = slice(side + chunk, side + chunk + CHUNK)
            source = pl.ds(row + chunk, CHUNK)
            obj = []
            for plane in range(2):
                rolled = [
                    pltpu.roll(field[plane, block + j, source, :], back_shift, 1)
                    for j in range(3)
                ]
                obj.append(
                    [jnp.where(lane < LANES - off, rolled[j], rolled[j + 1]) for j in range(2)]
                )
            for j in range(2):
                cols = slice(j * LANES, (j + 1) * LANES)
                obj_re, obj_im = obj[0][j], obj[1][j]
                patch[0, rows, cols] = obj_re
                patch[1, rows, cols] = obj_im
                for m in range(2):
                    probe_re = probe_f32[m, rows, cols]
                    probe_im = probe_f32[m, rows, side + j * LANES : side + (j + 1) * LANES]
                    out = slice(m * side + j * LANES, m * side + (j + 1) * LANES)
                    wave[rows, out] = (probe_re * obj_re - probe_im * obj_im).astype(jnp.bfloat16)
                    wave[low, out] = (probe_re * obj_im + probe_im * obj_re).astype(jnp.bfloat16)

        return [functools.partial(step, chunk) for chunk in chunks]

    def left(k, table):
        wave, half = waves[k], halves[k]

        def step(m):
            cols = slice(m * side, (m + 1) * side)
            stacked = jnp.dot(table[...], wave[:, cols], preferred_element_type=jnp.float32)
            half[cols, :side] = stacked[:side].astype(jnp.bfloat16)
            half[cols, side:] = stacked[side:].astype(jnp.bfloat16)

        return [functools.partial(step, m) for m in range(2)]

    def right(k, table):
        half, far = halves[k], fars[k]

        def step(m):
            rows = slice(m * side, (m + 1) * side)
            far[rows] = jnp.dot(half[rows], table[...], preferred_element_type=jnp.float32)

        return [functools.partial(step, m) for m in range(2)]

    def compare(k, slot):
        far, wave = fars[k], waves[k]
        valid = jnp.where(slot < total, 1.0, 0.0)

        def step(chunk):
            parts = []
            power = 1.0
            for m in range(2):
                rows = slice(m * side + chunk, m * side + chunk + CHUNK)
                far_re, far_im = far[rows, :side], far[rows, side:]
                power = power + (far_re * far_re + far_im * far_im)
                parts.append((far_re, far_im))
            level = inten[jnp.clip(slot, 0, slots - 1), chunk : chunk + CHUNK]
            level = level.astype(jnp.float32) + 1.0
            ratio = valid - (valid * level) * lax.rsqrt(level * power)
            for m in range(2):
                cols = slice(m * side, (m + 1) * side)
                wave[chunk : chunk + CHUNK, cols] = (parts[m][0] * ratio).astype(jnp.bfloat16)
                wave[side + chunk : side + chunk + CHUNK, cols] = (parts[m][1] * ratio).astype(
                    jnp.bfloat16
                )

        return [functools.partial(step, chunk) for chunk in chunks]

    def gather(k, slot):
        row, block, off = spot(slot)
        far, patch = fars[k], patches[k]

        def step(chunk):
            rows = slice(chunk, chunk + CHUNK)
            obj_re, obj_im = patch[0, rows], patch[1, rows]
            terms = [0.0, 0.0]
            for m in range(2):
                probe_re = probe_f32[m, rows, :side]
                probe_im = probe_f32[m, rows, side:]
                far_rows = slice(m * side + chunk, m * side + chunk + CHUNK)
                back_re, back_im = far[far_rows, :side], far[far_rows, side:]
                terms[0] = terms[0] + (probe_re * back_re + probe_im * back_im)
                terms[1] = terms[1] + (probe_re * back_im - probe_im * back_re)
                probe_grad[m, rows, :side] += obj_re * back_re + obj_im * back_im
                probe_grad[m, rows, side:] += obj_re * back_im - obj_im * back_re
            target = pl.ds(row + chunk, CHUNK)
            for plane in range(2):
                first = pltpu.roll(terms[plane][:, :LANES], off, 1)
                second = pltpu.roll(terms[plane][:, LANES:], off, 1)
                grad[block, plane, target, :] += jnp.where(lane < off, 0.0, first)
                grad[block + 1, plane, target, :] += jnp.where(lane < off, first, second)
                grad[block + 2, plane, target, :] += jnp.where(lane < off, second, 0.0)

        return [functools.partial(step, chunk) for chunk in chunks]

    for step in cut(0, 0):
        step()

    @pl.loop(0, (total + 1) // 2)
    def pair(index):
        slot = 2 * index
        interleave(left(0, plain) + right(0, turned), gather(1, slot - 1) + cut(1, slot + 1))
        interleave(left(1, plain) + right(1, turned), compare(0, slot))
        interleave(left(0, turned) + right(0, plain), compare(1, slot + 1))
        interleave(left(1, turned) + right(1, plain), gather(0, slot) + cut(0, slot + 2))

    for step in gather(1, 2 * ((total + 1) // 2) - 1):
        step()

    width = blocks // owners
    sends = []

    def send(src, dst):
        sends.append(pltpu.make_async_copy(src, dst, out_sems.at[len(sends)]))

    send(probe_grad.at[1 - mode], give_probe)
    send(probe_grad.at[mode], keep_probe)
    for step in list(range(1, owners // 2)) + [0]:
        owner = 2 * lax.rem(sub + step, owners // 2)
        for part, target in (
            (owner + 1 - mode, give_others if step else give_mine),
            (owner + mode, keep_others if step else keep_mine),
        ):
            if step:
                target = target.at[pl.ds((step - 1) * width, width)]
            send(grad.at[pl.ds(part * width, width)], target)
    for copy in sends:
        copy.start()
    for copy in sends:
        copy.wait()


def prepare_kernel(probe, inten, plain, turned, *outs):
    probe_f32 = outs[0]
    probe_f32[...] = probe[...].astype(jnp.float32)
    for source, target in zip((inten, plain, turned), outs[1:]):
        target[...] = source[...]


def prepare(probe, inten):
    tables = [jnp.asarray(x) for x in dft_tables(probe.shape[1])]
    return small_kernel(
        prepare_kernel,
        [shape(*probe.shape)]
        + [jax.ShapeDtypeStruct(x.shape, x.dtype) for x in (inten, *tables)],
        probe,
        inten,
        *tables,
        name="prepare",
    )


def point_sums(place, counts, spots, own, halos, prepared, owners):
    probe, inten, plain, turned = prepared
    side = probe.shape[1]
    blocks = own.shape[2] // LANES
    rows = own.shape[1] + side
    width = blocks // owners

    def piece(count):
        return jax.ShapeDtypeStruct((count, 2, rows, LANES), jnp.float32)

    mode_sum = jax.ShapeDtypeStruct((side, 2 * side), jnp.float32)
    smem = pl.BlockSpec(memory_space=pltpu.SMEM)
    vmem = pl.BlockSpec(memory_space=pltpu.VMEM)
    anywhere = pl.BlockSpec(memory_space=pl.ANY)
    slots = inten.shape[0]
    return pl.pallas_call(
        functools.partial(point_kernel, owners=owners),
        out_shape=[piece(width)] * 2 + [piece(blocks // 2 - width)] * 2 + [mode_sum] * 2,
        in_specs=[smem] * 3 + [anywhere] * 5 + [vmem] * 4,
        out_specs=[anywhere] * 6,
        scratch_shapes=[
            pltpu.VMEM((2, blocks + 1, rows, LANES), jnp.float32),
            pltpu.VMEM((blocks + 1, 2, rows, LANES), jnp.float32),
            pltpu.VMEM((2, side, 2 * side), jnp.float32),
            *[pltpu.VMEM((2, side, side), jnp.float32)] * 2,
            *[pltpu.VMEM((2 * side, 2 * side), jnp.bfloat16)] * 4,
            *[pltpu.VMEM((2 * side, 2 * side), jnp.float32)] * 2,
            pltpu.SemaphoreType.DMA((6 * blocks,)),
            pltpu.SemaphoreType.DMA((owners + 2,)),
        ],
        compiler_params=pltpu.CompilerParams(vmem_limit_bytes=24 * 1024 * 1024),
        cost_estimate=pl.CostEstimate(
            flops=slots * 32 * 2 * side**3, bytes_accessed=16 * 1024 * 1024, transcendentals=0
        ),
        name="point_sums",
    )(place, counts, spots, own, *halos, *prepared)


def with_neighbours(first, second):
    count = lax.axis_size("tiles")
    pairs = [(i, i + 1) for i in range(count - 1)]
    return [
        lax.ppermute(cells, "tiles", [x for a, b in pairs[turn::2] for x in ((a, b), (b, a))])
        for turn, cells in enumerate((first, second))
    ]


def swap(cells):
    return lax.ppermute(cells, "modes", [(0, 1), (1, 0)])


def rotated(cells, axis, step):
    count = lax.axis_size(axis)
    return lax.ppermute(cells, axis, [(i, (i + step) % count) for i in range(count)])


def small_kernel(body, out_shape, *args, name):
    return pl.pallas_call(
        body,
        out_shape=out_shape,
        in_specs=[
            pl.BlockSpec(memory_space=pltpu.SMEM if x.dtype == jnp.int32 else pltpu.VMEM)
            for x in args
        ],
        out_specs=jax.tree.map(lambda _: pl.BlockSpec(memory_space=pltpu.VMEM), out_shape),
        compiler_params=pltpu.CompilerParams(vmem_limit_bytes=24 * 1024 * 1024),
        cost_estimate=pl.CostEstimate(flops=0, bytes_accessed=0, transcendentals=0),
        name=name,
    )(*args)


def shape(*dims):
    return jax.ShapeDtypeStruct(dims, jnp.float32)


def after(cells, *earlier):
    return lax.optimization_barrier((cells, *earlier))[0]


def add_kernel(*refs):
    total = refs[0][...]
    for ref in refs[1:-1]:
        total = total + ref[...]
    refs[-1][...] = total


def others_kernel(kept, got, *outs):
    width, _, rows = outs[1].shape[:3]
    rim = outs[0].shape[2] // 2
    for step in range(len(outs) // 2):
        rims, core = outs[2 * step : 2 * step + 2]
        cut = slice(step * width, (step + 1) * width)
        rims[:, :, :rim] = kept[cut, :, :rim] + got[cut, :, :rim]
        rims[:, :, rim:] = kept[cut, :, rim + rows :] + got[cut, :, rim + rows :]
        core[...] = kept[cut, :, rim : rim + rows] + got[cut, :, rim : rim + rows]


def mine_kernel(place, kept, got, *rest):
    first, core, second = rest[-3:]
    rim, rows = first.shape[2], core.shape[2]
    total_above = kept[:, :, :rim] + got[:, :, :rim]
    total_below = kept[:, :, rim + rows :] + got[:, :, rim + rows :]
    for other in rest[:-3]:
        total_above = total_above + other[:, :, :rim]
        total_below = total_below + other[:, :, rim:]
    even = place[0] % 2 == 0

    @pl.when(even)
    def below_first():
        first[...] = total_below
        second[...] = total_above

    @pl.when(~even)
    def above_first():
        first[...] = total_above
        second[...] = total_below

    core[...] = kept[:, :, rim : rim + rows] + got[:, :, rim : rim + rows]


def fold_kernel(place, core, first, second, out):
    rim, rows = first.shape[2], core.shape[2]
    out[...] = core[...]
    near = pl.multiple_of((place[0] % 2) * (rows - rim), 8)
    far = pl.multiple_of(rows - rim - near, 8)
    out[:, :, pl.ds(far, rim)] += first[...]
    out[:, :, pl.ds(near, rim)] += second[...]


def finish_kernel(core, *rest):
    out = rest[-1]
    for block in range(core.shape[0]):
        total = core[block]
        for other in rest[:-1]:
            total = total + other[block]
        out[:, :, block * LANES : (block + 1) * LANES] = total


def share_rows(index, share):
    return pl.ds(pl.multiple_of(index * share, share), share)


def shares_kernel(place, kept, got, *outs):
    share = outs[0].shape[0]
    for step, out in enumerate(outs):
        rows = share_rows(place[0] ^ step, share)
        out[...] = kept[rows] + got[rows]


def order_kernel(place, *refs):
    out = refs[-1]
    share = refs[0].shape[0]
    for step, part in enumerate(refs[:-1]):
        out[share_rows(place[0] ^ step, share)] = part[...]


def both_kernel(place, mine, other, out):
    out[place[2]] = mine[...]
    out[1 - place[2]] = other[...]


def on_device(object_field, probe, intensity, centres, counts):
    side = probe.shape[1]
    rim = side // 2
    strip_rows, cols = object_field.shape[1:]
    strip = lax.axis_index("tiles")
    sub = lax.axis_index("sub")
    mode = lax.axis_index("modes")
    tiles, subs = lax.axis_size("tiles"), lax.axis_size("sub")
    owners = subs * lax.axis_size("modes")
    width = cols // owners // LANES
    place = jnp.stack([strip, sub, mode]).astype(jnp.int32)

    last = strip_rows - rim
    even = strip % 2 == 0
    ends = [
        lax.dynamic_slice(object_field, (mode, jnp.where(at_end, last, 0), 0), (1, rim, cols))[0]
        for at_end in (even, ~even)
    ]
    first, second = with_neighbours(*ends)
    halos = (first, second, swap(first), swap(second))

    keep_mine, give_mine, keep_others, give_others, keep_probe, give_probe = point_sums(
        place, counts, centres.reshape(-1), object_field, halos, prepare(probe, intensity[0]), owners
    )
    got_probe = swap(give_probe)
    got_others = swap(give_others)
    got_mine = swap(give_mine)

    rims_shape = shape(width, 2, 2 * rim, LANES)
    core_shape = shape(width, 2, strip_rows, LANES)
    outgoing = list(small_kernel(
        others_kernel,
        [rims_shape, core_shape] * (subs - 1),
        keep_others,
        got_others,
        name="object_others",
    ))

    def rotate_all(parts):
        return [rotated(x, "sub", step + 1) for step, x in enumerate(parts)]

    def rotate_strips(parts):
        return [
            lax.ppermute(x, "tiles", [(i, i ^ (step + 1)) for i in range(tiles)])
            for step, x in enumerate(parts)
        ]

    direct = tiles in (1, 2, 4)
    total_rows, total_cols = keep_probe.shape
    share = shape(total_rows // tiles, total_cols)
    if direct:
        parts = small_kernel(
            shares_kernel, [share] * tiles, place, keep_probe, got_probe, name="probe_shares"
        )
        parts_in = rotate_strips(parts[1:])
    rims_in = rotate_all(outgoing[0::2])
    core_out = outgoing[1::2]
    first, core, second = small_kernel(
        mine_kernel,
        [shape(width, 2, rim, LANES), core_shape, shape(width, 2, rim, LANES)],
        place,
        keep_mine,
        got_mine,
        *rims_in,
        name="object_mine",
    )
    if direct:
        part_sum = small_kernel(add_kernel, share, parts[0], *parts_in, name="probe_strips_sum")
        part_sum, first, second = lax.optimization_barrier((part_sum, first, second))
        part_in = [rotated(part_sum, "sub", step) for step in range(1, subs)]
    first, second = with_neighbours(first, second)
    folded = small_kernel(
        fold_kernel, core_shape, place, core, first, second, name="object_fold"
    )
    if direct:
        part_sum = small_kernel(add_kernel, share, part_sum, *part_in, name="probe_total")
        part_sum, folded, *core_out = lax.optimization_barrier((part_sum, folded, *core_out))
        parts_in = rotate_strips([part_sum] * (tiles - 1))
    core_in = rotate_all(core_out)
    if direct:
        probe_mine = small_kernel(
            order_kernel,
            shape(total_rows, total_cols),
            place,
            part_sum,
            *parts_in,
            name="probe_order",
        )
    else:
        probe_mine = lax.psum(keep_probe + got_probe, ("tiles", "sub"))
    object_grad = small_kernel(
        finish_kernel,
        shape(2, strip_rows, width * LANES),
        folded,
        *core_in,
        name="object_finish",
    )
    probe_grad = small_kernel(
        both_kernel,
        shape(2, *probe_mine.shape),
        place,
        probe_mine,
        swap(probe_mine),
        name="probe_both",
    )
    return (object_grad, probe_grad)


def solution(mesh):
    return jax.shard_map(
        on_device,
        mesh=mesh,
        in_specs=(
            P(None, ("groups", "tiles"), None),
            P("groups", None, None),
            P(("groups", "tiles"), ("sub", "modes"), None, None),
            P(("groups", "tiles"), None, None),
            P(("groups", "tiles")),
        ),
        out_specs=(P(None, ("groups", "tiles"), ("sub", "modes")), P("groups", None, None)),
        check_vma=False,
    )
```

```python
import functools
import math

import jax
import jax.numpy as jnp
import ml_dtypes
import numpy as np
from jax import lax
from jax.experimental import pallas as pl
from jax.experimental.pallas import tpu as pltpu
from jax.sharding import PartitionSpec as P

LANES = 128
CHUNK = 64


def dft_tables(size):
    index = np.arange(size)
    angle = (index[:, None] * index[None, :] % size) * (2.0 * math.pi / size)
    scale = 1.0 / math.sqrt(size)
    cos_part = (np.cos(angle) * scale).astype(np.float32).astype(ml_dtypes.bfloat16)
    sin_part = (-np.sin(angle) * scale).astype(np.float32).astype(ml_dtypes.bfloat16)
    return np.concatenate([cos_part, sin_part])


def interleave(first, second):
    done = 0
    for index, step in enumerate(first):
        step()
        upto = (index + 1) * len(second) // len(first)
        for other in second[done:upto]:
            other()
        done = upto


def point_kernel(
    place,
    counts,
    spots,
    own,
    first_a,
    second_a,
    first_b,
    second_b,
    probe_f32,
    inten,
    plain,
    turned,
    *rest,
    owners,
):
    keep_mine, give_mine, keep_others, give_others, keep_probe, give_probe = rest[:6]
    field, grad, probe_grad = rest[6:9]
    patches, waves, halves, fars = (rest[9 + 2 * i : 11 + 2 * i] for i in range(4))
    sems, out_sems = rest[17:]
    strip, sub, mode = place[0], place[1], place[2]
    member = sub * 2 + mode
    side = probe_f32.shape[1]
    rim = side // 2
    strip_rows = own.shape[1]
    blocks = own.shape[2] // LANES
    slots = inten.shape[0]
    total = jnp.clip(counts[0] - member * slots, 0, slots)
    far_rows = rim + strip_rows
    near = (strip % 2) * far_rows
    copies = []

    def fetch(src, dst):
        copies.append(pltpu.make_async_copy(src, dst, sems.at[len(copies)]))

    for block in range(blocks):
        cols = pl.ds(block * LANES, LANES)
        for plane in range(2):
            fetch(own.at[plane, :, cols], field.at[plane, block, pl.ds(rim, strip_rows)])
        for first, second, plane in ((first_a, second_a, mode), (first_b, second_b, 1 - mode)):
            fetch(first.at[:, cols], field.at[plane, block, pl.ds(far_rows - near, rim)])
            fetch(second.at[:, cols], field.at[plane, block, pl.ds(near, rim)])
    for copy in copies:
        copy.start()

    probe_grad[...] = jnp.zeros_like(probe_grad)
    patches[1][...] = jnp.zeros_like(patches[1])
    fars[1][...] = jnp.zeros_like(fars[1])

    @pl.loop(0, grad.shape[0])
    def clear(block):
        grad[block] = jnp.zeros(grad.shape[1:], jnp.float32)

    for copy in copies:
        copy.wait()

    lane = lax.broadcasted_iota(jnp.int32, (CHUNK, LANES), 1)
    chunks = range(0, side, CHUNK)

    def spot(slot):
        base = 2 * (member * slots + jnp.clip(slot, 0, slots - 1))
        row = spots[base] - strip * strip_rows
        col = spots[base + 1] - rim
        return row, col // LANES, col % LANES

    def cut(k, slot):
        row, block, off = spot(slot)
        back_shift = (LANES - off) % LANES
        patch, wave = patches[k], waves[k]

        def step(chunk):
            rows = slice(chunk, chunk + CHUNK)
            low = slice(side + chunk, side + chunk + CHUNK)
            source = pl.ds(row + chunk, CHUNK)
            obj = []
            for plane in range(2):
                rolled = [
                    pltpu.roll(field[plane, block + j, source, :], back_shift, 1)
                    for j in range(3)
                ]
                obj.append(
                    [jnp.where(lane < LANES - off, rolled[j], rolled[j + 1]) for j in range(2)]
                )
            for j in range(2):
                cols = slice(j * LANES, (j + 1) * LANES)
                obj_re, obj_im = obj[0][j], obj[1][j]
                patch[0, rows, cols] = obj_re
                patch[1, rows, cols] = obj_im
                for m in range(2):
                    probe_re = probe_f32[m, rows, cols]
                    probe_im = probe_f32[m, rows, side + j * LANES : side + (j + 1) * LANES]
                    out = slice(m * side + j * LANES, m * side + (j + 1) * LANES)
                    wave[rows, out] = (probe_re * obj_re - probe_im * obj_im).astype(jnp.bfloat16)
                    wave[low, out] = (probe_re * obj_im + probe_im * obj_re).astype(jnp.bfloat16)

        return [functools.partial(step, chunk) for chunk in chunks]

    def left(k, table):
        wave, half = waves[k], halves[k]

        def step(m):
            cols = slice(m * side, (m + 1) * side)
            stacked = jnp.dot(table[...], wave[:, cols], preferred_element_type=jnp.float32)
            half[cols, :side] = stacked[:side].astype(jnp.bfloat16)
            half[cols, side:] = stacked[side:].astype(jnp.bfloat16)

        return [functools.partial(step, m) for m in range(2)]

    def right(k, table):
        half, far = halves[k], fars[k]

        def step(m):
            rows = slice(m * side, (m + 1) * side)
            far[rows] = jnp.dot(half[rows], table[...], preferred_element_type=jnp.float32)

        return [functools.partial(step, m) for m in range(2)]

    def compare(k, slot):
        far, wave = fars[k], waves[k]
        valid = jnp.where(slot < total, 1.0, 0.0)

        def step(chunk):
            parts = []
            power = 1.0
            for m in range(2):
                rows = slice(m * side + chunk, m * side + chunk + CHUNK)
                far_re, far_im = far[rows, :side], far[rows, side:]
                power = power + (far_re * far_re + far_im * far_im)
                parts.append((far_re, far_im))
            level = inten[jnp.clip(slot, 0, slots - 1), chunk : chunk + CHUNK]
            level = level.astype(jnp.float32) + 1.0
            ratio = valid - (valid * level) * lax.rsqrt(level * power)
            for m in range(2):
                cols = slice(m * side, (m + 1) * side)
                wave[chunk : chunk + CHUNK, cols] = (parts[m][0] * ratio).astype(jnp.bfloat16)
                wave[side + chunk : side + chunk + CHUNK, cols] = (parts[m][1] * ratio).astype(
                    jnp.bfloat16
                )

        return [functools.partial(step, chunk) for chunk in chunks]

    def gather(k, slot):
        row, block, off = spot(slot)
        far, patch = fars[k], patches[k]

        def step(chunk):
            rows = slice(chunk, chunk + CHUNK)
            obj_re, obj_im = patch[0, rows], patch[1, rows]
            terms = [0.0, 0.0]
            for m in range(2):
                probe_re = probe_f32[m, rows, :side]
                probe_im = probe_f32[m, rows, side:]
                far_rows = slice(m * side + chunk, m * side + chunk + CHUNK)
                back_re, back_im = far[far_rows, :side], far[far_rows, side:]
                terms[0] = terms[0] + (probe_re * back_re + probe_im * back_im)
                terms[1] = terms[1] + (probe_re * back_im - probe_im * back_re)
                probe_grad[m, rows, :side] += obj_re * back_re + obj_im * back_im
                probe_grad[m, rows, side:] += obj_re * back_im - obj_im * back_re
            target = pl.ds(row + chunk, CHUNK)
            for plane in range(2):
                first = pltpu.roll(terms[plane][:, :LANES], off, 1)
                second = pltpu.roll(terms[plane][:, LANES:], off, 1)
                grad[block, plane, target, :] += jnp.where(lane < off, 0.0, first)
                grad[block + 1, plane, target, :] += jnp.where(lane < off, first, second)
                grad[block + 2, plane, target, :] += jnp.where(lane < off, second, 0.0)

        return [functools.partial(step, chunk) for chunk in chunks]

    for step in cut(0, 0):
        step()

    @pl.loop(0, (total + 1) // 2)
    def pair(index):
        slot = 2 * index
        interleave(left(0, plain) + right(0, turned), gather(1, slot - 1) + cut(1, slot + 1))
        interleave(left(1, plain) + right(1, turned), compare(0, slot))
        interleave(left(0, turned) + right(0, plain), compare(1, slot + 1))
        interleave(left(1, turned) + right(1, plain), gather(0, slot) + cut(0, slot + 2))

    for step in gather(1, 2 * ((total + 1) // 2) - 1):
        step()

    width = blocks // owners
    sends = []

    def send(src, dst):
        sends.append(pltpu.make_async_copy(src, dst, out_sems.at[len(sends)]))

    send(probe_grad.at[1 - mode], give_probe)
    send(probe_grad.at[mode], keep_probe)
    for step in list(range(1, owners // 2)) + [0]:
        owner = 2 * lax.rem(sub + step, owners // 2)
        for part, target in (
            (owner + 1 - mode, give_others if step else give_mine),
            (owner + mode, keep_others if step else keep_mine),
        ):
            if step:
                target = target.at[pl.ds((step - 1) * width, width)]
            send(grad.at[pl.ds(part * width, width)], target)
    for copy in sends:
        copy.start()
    for copy in sends:
        copy.wait()


def prepare_kernel(probe, inten_in, table, probe_f32, inten, plain, turned):
    side = table.shape[1]
    cos_part, sin_part = table[:side], table[side:]
    probe_f32[...] = probe[...].astype(jnp.float32)
    inten[...] = inten_in[...]
    for target, first, second in ((plain, -sin_part, sin_part), (turned, sin_part, -sin_part)):
        target[:side, :side] = cos_part
        target[side:, side:] = cos_part
        target[:side, side:] = first
        target[side:, :side] = second


def prepare(probe, inten):
    side = probe.shape[1]
    table = jnp.asarray(dft_tables(side))
    square = jax.ShapeDtypeStruct((2 * side, 2 * side), table.dtype)
    return small_kernel(
        prepare_kernel,
        [shape(*probe.shape), jax.ShapeDtypeStruct(inten.shape, inten.dtype), square, square],
        probe,
        inten,
        table,
        name="prepare",
    )


def point_sums(place, counts, spots, own, halos, prepared, owners):
    probe, inten, plain, turned = prepared
    side = probe.shape[1]
    blocks = own.shape[2] // LANES
    rows = own.shape[1] + side
    width = blocks // owners

    def piece(count):
        return jax.ShapeDtypeStruct((count, 2, rows, LANES), jnp.float32)

    mode_sum = jax.ShapeDtypeStruct((side, 2 * side), jnp.float32)
    smem = pl.BlockSpec(memory_space=pltpu.SMEM)
    vmem = pl.BlockSpec(memory_space=pltpu.VMEM)
    anywhere = pl.BlockSpec(memory_space=pl.ANY)
    slots = inten.shape[0]
    return pl.pallas_call(
        functools.partial(point_kernel, owners=owners),
        out_shape=[piece(width)] * 2 + [piece(blocks // 2 - width)] * 2 + [mode_sum] * 2,
        in_specs=[smem] * 3 + [anywhere] * 5 + [vmem] * 4,
        out_specs=[anywhere] * 6,
        scratch_shapes=[
            pltpu.VMEM((2, blocks + 1, rows, LANES), jnp.float32),
            pltpu.VMEM((blocks + 1, 2, rows, LANES), jnp.float32),
            pltpu.VMEM((2, side, 2 * side), jnp.float32),
            *[pltpu.VMEM((2, side, side), jnp.float32)] * 2,
            *[pltpu.VMEM((2 * side, 2 * side), jnp.bfloat16)] * 4,
            *[pltpu.VMEM((2 * side, 2 * side), jnp.float32)] * 2,
            pltpu.SemaphoreType.DMA((6 * blocks,)),
            pltpu.SemaphoreType.DMA((owners + 2,)),
        ],
        compiler_params=pltpu.CompilerParams(vmem_limit_bytes=24 * 1024 * 1024),
        cost_estimate=pl.CostEstimate(
            flops=slots * 32 * 2 * side**3, bytes_accessed=16 * 1024 * 1024, transcendentals=0
        ),
        name="point_sums",
    )(place, counts, spots, own, *halos, *prepared)


def with_neighbours(first, second):
    count = lax.axis_size("tiles")
    pairs = [(i, i + 1) for i in range(count - 1)]
    return [
        lax.ppermute(cells, "tiles", [x for a, b in pairs[turn::2] for x in ((a, b), (b, a))])
        for turn, cells in enumerate((first, second))
    ]


def swap(cells):
    return lax.ppermute(cells, "modes", [(0, 1), (1, 0)])


def rotated(cells, axis, step):
    count = lax.axis_size(axis)
    return lax.ppermute(cells, axis, [(i, (i + step) % count) for i in range(count)])


def small_kernel(body, out_shape, *args, name):
    return pl.pallas_call(
        body,
        out_shape=out_shape,
        in_specs=[
            pl.BlockSpec(memory_space=pltpu.SMEM if x.dtype == jnp.int32 else pltpu.VMEM)
            for x in args
        ],
        out_specs=jax.tree.map(lambda _: pl.BlockSpec(memory_space=pltpu.VMEM), out_shape),
        compiler_params=pltpu.CompilerParams(vmem_limit_bytes=4 * 1024 * 1024),
        cost_estimate=pl.CostEstimate(flops=0, bytes_accessed=0, transcendentals=0),
        name=name,
    )(*args)


def shape(*dims):
    return jax.ShapeDtypeStruct(dims, jnp.float32)


def after(cells, *earlier):
    return lax.optimization_barrier((cells, *earlier))[0]


def add_kernel(*refs):
    total = refs[0][...]
    for ref in refs[1:-1]:
        total = total + ref[...]
    refs[-1][...] = total


def others_kernel(kept, got, *outs):
    width, _, rows = outs[1].shape[:3]
    rim = outs[0].shape[2] // 2
    for step in range(len(outs) // 2):
        rims, core = outs[2 * step : 2 * step + 2]
        cut = slice(step * width, (step + 1) * width)
        rims[:, :, :rim] = kept[cut, :, :rim] + got[cut, :, :rim]
        rims[:, :, rim:] = kept[cut, :, rim + rows :] + got[cut, :, rim + rows :]
        core[...] = kept[cut, :, rim : rim + rows] + got[cut, :, rim : rim + rows]


def mine_kernel(place, kept, got, *rest):
    first, core, second = rest[-3:]
    rim, rows = first.shape[2], core.shape[2]
    total_above = kept[:, :, :rim] + got[:, :, :rim]
    total_below = kept[:, :, rim + rows :] + got[:, :, rim + rows :]
    for other in rest[:-3]:
        total_above = total_above + other[:, :, :rim]
        total_below = total_below + other[:, :, rim:]
    even = place[0] % 2 == 0

    @pl.when(even)
    def below_first():
        first[...] = total_below
        second[...] = total_above

    @pl.when(~even)
    def above_first():
        first[...] = total_above
        second[...] = total_below

    core[...] = kept[:, :, rim : rim + rows] + got[:, :, rim : rim + rows]


def finish_kernel(place, core, first, second, *rest):
    out = rest[-1]
    rim, rows = first.shape[2], core.shape[2]
    near = pl.multiple_of((place[0] % 2) * (rows - rim), 8)
    far = pl.multiple_of(rows - rim - near, 8)
    for block in range(core.shape[0]):
        total = core[block]
        for other in rest[:-1]:
            total = total + other[block]
        cols = slice(block * LANES, (block + 1) * LANES)
        out[:, :, cols] = total
        out[:, pl.ds(far, rim), cols] += first[block]
        out[:, pl.ds(near, rim), cols] += second[block]


def share_rows(index, share):
    return pl.ds(pl.multiple_of(index * share, share), share)


def shares_kernel(place, kept, got, *outs):
    share = outs[0].shape[0]
    for step, out in enumerate(outs):
        rows = share_rows(place[0] ^ step, share)
        out[...] = kept[rows] + got[rows]


def gather_kernel(place, *refs):
    out, sems = refs[-2:]
    parts = refs[:-2]
    tiles = len(parts) // 2
    share = parts[0].shape[0]
    copies = []
    for index, part in enumerate(parts):
        swapped, step = divmod(index, tiles)
        mode = place[2] if swapped == 0 else 1 - place[2]
        target = out.at[mode, share_rows(place[0] ^ step, share)]
        copies.append(pltpu.make_async_copy(part, target, sems.at[index]))
    for copy in copies:
        copy.start()
    for copy in copies:
        copy.wait()


def gather_parts(place, parts):
    tiles = len(parts) // 2
    share, width = parts[0].shape
    return pl.pallas_call(
        gather_kernel,
        out_shape=shape(2, tiles * share, width),
        in_specs=[pl.BlockSpec(memory_space=pltpu.SMEM)]
        + [pl.BlockSpec(memory_space=pltpu.VMEM)] * len(parts),
        out_specs=pl.BlockSpec(memory_space=pl.ANY),
        scratch_shapes=[pltpu.SemaphoreType.DMA((len(parts),))],
        compiler_params=pltpu.CompilerParams(vmem_limit_bytes=4 * 1024 * 1024),
        name="probe_gather",
    )(place, *parts)


def on_device(object_field, probe, intensity, centres, counts):
    side = probe.shape[1]
    rim = side // 2
    strip_rows, cols = object_field.shape[1:]
    strip = lax.axis_index("tiles")
    sub = lax.axis_index("sub")
    mode = lax.axis_index("modes")
    tiles, subs = lax.axis_size("tiles"), lax.axis_size("sub")
    owners = subs * lax.axis_size("modes")
    width = cols // owners // LANES
    place = jnp.stack([strip, sub, mode]).astype(jnp.int32)

    last = strip_rows - rim
    even = strip % 2 == 0
    ends = [
        lax.dynamic_slice(object_field, (mode, jnp.where(at_end, last, 0), 0), (1, rim, cols))[0]
        for at_end in (even, ~even)
    ]
    first, second = with_neighbours(*ends)
    halos = (first, second, swap(first), swap(second))

    keep_mine, give_mine, keep_others, give_others, keep_probe, give_probe = point_sums(
        place, counts, centres.reshape(-1), object_field, halos, prepare(probe, intensity[0]), owners
    )
    got_probe = swap(give_probe)
    got_others = swap(give_others)
    got_mine = swap(give_mine)

    rims_shape = shape(width, 2, 2 * rim, LANES)
    core_shape = shape(width, 2, strip_rows, LANES)
    direct = tiles in (1, 2, 4)
    total_rows, total_cols = keep_probe.shape
    share = shape(total_rows // tiles, total_cols)
    if direct:
        parts = small_kernel(
            shares_kernel, [share] * tiles, place, keep_probe, got_probe, name="probe_shares"
        )
        got_others, *parts = lax.optimization_barrier((got_others, *parts))
    outgoing = list(small_kernel(
        others_kernel,
        [rims_shape, core_shape] * (subs - 1),
        keep_others,
        got_others,
        name="object_others",
    ))

    def rotate_all(parts):
        return [rotated(x, "sub", step + 1) for step, x in enumerate(parts)]

    def rotate_strips(parts):
        return [
            lax.ppermute(x, "tiles", [(i, i ^ (step + 1)) for i in range(tiles)])
            for step, x in enumerate(parts)
        ]

    if direct:
        parts_in = rotate_strips(parts[1:])
    rims_in = rotate_all(outgoing[0::2])
    core_out = outgoing[1::2]
    first, core, second = small_kernel(
        mine_kernel,
        [shape(width, 2, rim, LANES), core_shape, shape(width, 2, rim, LANES)],
        place,
        keep_mine,
        got_mine,
        *rims_in,
        name="object_mine",
    )
    if direct:
        part_sum = small_kernel(add_kernel, share, parts[0], *parts_in, name="probe_strips_sum")
        part_sum, first, second = lax.optimization_barrier((part_sum, first, second))
        part_in = [rotated(part_sum, "sub", step) for step in range(1, subs)]
    first, second = with_neighbours(first, second)
    if direct:
        part_sum = small_kernel(add_kernel, share, part_sum, *part_in, name="probe_total")
        part_sum, core, *core_out = lax.optimization_barrier((part_sum, core, *core_out))
        parts_in = rotate_strips([part_sum] * (tiles - 1))
    core_in = rotate_all(core_out)
    object_grad = small_kernel(
        finish_kernel,
        shape(2, strip_rows, width * LANES),
        place,
        core,
        first,
        second,
        *core_in,
        name="object_finish",
    )
    if direct:
        parts = [part_sum, *parts_in]
    else:
        parts = [lax.psum(keep_probe + got_probe, ("tiles", "sub"))]
    spot = place if direct else place * jnp.array([0, 0, 1], jnp.int32)
    probe_grad = gather_parts(spot, [*parts, *[swap(x) for x in parts]])
    return (object_grad, probe_grad)


def solution(mesh):
    return jax.shard_map(
        on_device,
        mesh=mesh,
        in_specs=(
            P(None, ("groups", "tiles"), None),
            P("groups", None, None),
            P(("groups", "tiles"), ("sub", "modes"), None, None),
            P(("groups", "tiles"), None, None),
            P(("groups", "tiles")),
        ),
        out_specs=(P(None, ("groups", "tiles"), ("sub", "modes")), P("groups", None, None)),
        check_vma=False,
    )
```

```python
import functools
import math

import jax
import jax.numpy as jnp
import ml_dtypes
import numpy as np
from jax import lax
from jax.experimental import pallas as pl
from jax.experimental.pallas import tpu as pltpu
from jax.sharding import PartitionSpec as P

LANES = 128
CHUNK = 64


def dft_tables(size):
    index = np.arange(size)
    angle = (index[:, None] * index[None, :] % size) * (2.0 * math.pi / size)
    scale = 1.0 / math.sqrt(size)
    cos_part = (np.cos(angle) * scale).astype(np.float32).astype(ml_dtypes.bfloat16)
    sin_part = (-np.sin(angle) * scale).astype(np.float32).astype(ml_dtypes.bfloat16)
    return np.concatenate([cos_part, sin_part])


def interleave(first, second):
    done = 0
    for index, step in enumerate(first):
        step()
        upto = (index + 1) * len(second) // len(first)
        for other in second[done:upto]:
            other()
        done = upto


def point_kernel(
    place,
    counts,
    spots,
    own,
    first_a,
    second_a,
    first_b,
    second_b,
    probe_f32,
    inten,
    plain,
    turned,
    *rest,
    owners,
):
    keep_mine, give_mine, keep_others, give_others, keep_probe, give_probe = rest[:6]
    field, grad, probe_grad = rest[6:9]
    patches, waves, halves, fars = (rest[9 + 2 * i : 11 + 2 * i] for i in range(4))
    sems, out_sems = rest[17:]
    strip, sub, mode = place[0], place[1], place[2]
    member = sub * 2 + mode
    side = probe_f32.shape[1]
    rim = side // 2
    strip_rows = own.shape[1]
    blocks = own.shape[2] // LANES
    slots = inten.shape[0]
    total = jnp.clip(counts[0] - member * slots, 0, slots)
    far_rows = rim + strip_rows
    near = (strip % 2) * far_rows
    copies = []

    def fetch(src, dst):
        copies.append(pltpu.make_async_copy(src, dst, sems.at[len(copies)]))

    for block in range(blocks):
        cols = pl.ds(block * LANES, LANES)
        for plane in range(2):
            fetch(own.at[plane, :, cols], field.at[plane, block, pl.ds(rim, strip_rows)])
        for first, second, plane in ((first_a, second_a, mode), (first_b, second_b, 1 - mode)):
            fetch(first.at[:, cols], field.at[plane, block, pl.ds(far_rows - near, rim)])
            fetch(second.at[:, cols], field.at[plane, block, pl.ds(near, rim)])
    for copy in copies:
        copy.start()

    probe_grad[...] = jnp.zeros_like(probe_grad)
    patches[1][...] = jnp.zeros_like(patches[1])
    fars[1][...] = jnp.zeros_like(fars[1])

    @pl.loop(0, grad.shape[0])
    def clear(block):
        grad[block] = jnp.zeros(grad.shape[1:], jnp.float32)

    for copy in copies:
        copy.wait()

    lane = lax.broadcasted_iota(jnp.int32, (CHUNK, LANES), 1)
    chunks = range(0, side, CHUNK)

    def spot(slot):
        base = 2 * (member * slots + jnp.clip(slot, 0, slots - 1))
        row = spots[base] - strip * strip_rows
        col = spots[base + 1] - rim
        return row, col // LANES, col % LANES

    def cut(k, slot):
        row, block, off = spot(slot)
        back_shift = (LANES - off) % LANES
        patch, wave = patches[k], waves[k]

        def step(chunk):
            rows = slice(chunk, chunk + CHUNK)
            low = slice(side + chunk, side + chunk + CHUNK)
            source = pl.ds(row + chunk, CHUNK)
            obj = []
            for plane in range(2):
                rolled = [
                    pltpu.roll(field[plane, block + j, source, :], back_shift, 1)
                    for j in range(3)
                ]
                obj.append(
                    [jnp.where(lane < LANES - off, rolled[j], rolled[j + 1]) for j in range(2)]
                )
            for j in range(2):
                cols = slice(j * LANES, (j + 1) * LANES)
                obj_re, obj_im = obj[0][j], obj[1][j]
                patch[0, rows, cols] = obj_re
                patch[1, rows, cols] = obj_im
                for m in range(2):
                    probe_re = probe_f32[m, rows, cols]
                    probe_im = probe_f32[m, rows, side + j * LANES : side + (j + 1) * LANES]
                    out = slice(m * side + j * LANES, m * side + (j + 1) * LANES)
                    wave[rows, out] = (probe_re * obj_re - probe_im * obj_im).astype(jnp.bfloat16)
                    wave[low, out] = (probe_re * obj_im + probe_im * obj_re).astype(jnp.bfloat16)

        return [functools.partial(step, chunk) for chunk in chunks]

    def left(k, table):
        wave, half = waves[k], halves[k]

        def step(m):
            cols = slice(m * side, (m + 1) * side)
            stacked = jnp.dot(table[...], wave[:, cols], preferred_element_type=jnp.float32)
            half[cols, :side] = stacked[:side].astype(jnp.bfloat16)
            half[cols, side:] = stacked[side:].astype(jnp.bfloat16)

        return [functools.partial(step, m) for m in range(2)]

    def right(k, table):
        half, far = halves[k], fars[k]

        def step(m):
            rows = slice(m * side, (m + 1) * side)
            far[rows] = jnp.dot(half[rows], table[...], preferred_element_type=jnp.float32)

        return [functools.partial(step, m) for m in range(2)]

    def compare(k, slot):
        far, wave = fars[k], waves[k]
        valid = jnp.where(slot < total, 1.0, 0.0)

        def step(chunk):
            parts = []
            power = 1.0
            for m in range(2):
                rows = slice(m * side + chunk, m * side + chunk + CHUNK)
                far_re, far_im = far[rows, :side], far[rows, side:]
                power = power + (far_re * far_re + far_im * far_im)
                parts.append((far_re, far_im))
            level = inten[jnp.clip(slot, 0, slots - 1), chunk : chunk + CHUNK]
            level = level.astype(jnp.float32) + 1.0
            ratio = valid - (valid * level) * lax.rsqrt(level * power)
            for m in range(2):
                cols = slice(m * side, (m + 1) * side)
                wave[chunk : chunk + CHUNK, cols] = (parts[m][0] * ratio).astype(jnp.bfloat16)
                wave[side + chunk : side + chunk + CHUNK, cols] = (parts[m][1] * ratio).astype(
                    jnp.bfloat16
                )

        return [functools.partial(step, chunk) for chunk in chunks]

    def gather(k, slot):
        row, block, off = spot(slot)
        far, patch = fars[k], patches[k]

        def step(chunk):
            rows = slice(chunk, chunk + CHUNK)
            obj_re, obj_im = patch[0, rows], patch[1, rows]
            terms = [0.0, 0.0]
            for m in range(2):
                probe_re = probe_f32[m, rows, :side]
                probe_im = probe_f32[m, rows, side:]
                far_rows = slice(m * side + chunk, m * side + chunk + CHUNK)
                back_re, back_im = far[far_rows, :side], far[far_rows, side:]
                terms[0] = terms[0] + (probe_re * back_re + probe_im * back_im)
                terms[1] = terms[1] + (probe_re * back_im - probe_im * back_re)
                probe_grad[m, rows, :side] += obj_re * back_re + obj_im * back_im
                probe_grad[m, rows, side:] += obj_re * back_im - obj_im * back_re
            target = pl.ds(row + chunk, CHUNK)
            for plane in range(2):
                first = pltpu.roll(terms[plane][:, :LANES], off, 1)
                second = pltpu.roll(terms[plane][:, LANES:], off, 1)
                grad[block, plane, target, :] += jnp.where(lane < off, 0.0, first)
                grad[block + 1, plane, target, :] += jnp.where(lane < off, first, second)
                grad[block + 2, plane, target, :] += jnp.where(lane < off, second, 0.0)

        return [functools.partial(step, chunk) for chunk in chunks]

    for step in cut(0, 0):
        step()

    @pl.loop(0, (total + 1) // 2)
    def pair(index):
        slot = 2 * index
        interleave(left(0, plain) + right(0, turned), gather(1, slot - 1) + cut(1, slot + 1))
        interleave(left(1, plain) + right(1, turned), compare(0, slot))
        interleave(left(0, turned) + right(0, plain), compare(1, slot + 1))
        interleave(left(1, turned) + right(1, plain), gather(0, slot) + cut(0, slot + 2))

    for step in gather(1, 2 * ((total + 1) // 2) - 1):
        step()

    width = blocks // owners
    sends = []

    def send(src, dst):
        sends.append(pltpu.make_async_copy(src, dst, out_sems.at[len(sends)]))

    send(probe_grad.at[1 - mode], give_probe)
    send(probe_grad.at[mode], keep_probe)
    for step in list(range(1, owners // 2)) + [0]:
        owner = 2 * lax.rem(sub + step, owners // 2)
        for part, target in (
            (owner + 1 - mode, give_others if step else give_mine),
            (owner + mode, keep_others if step else keep_mine),
        ):
            if step:
                target = target.at[pl.ds((step - 1) * width, width)]
            send(grad.at[pl.ds(part * width, width)], target)
    for copy in sends:
        copy.start()
    for copy in sends:
        copy.wait()


def prepare_kernel(probe, inten_in, table, probe_f32, inten, plain, turned):
    side = table.shape[1]
    cos_part, sin_part = table[:side], table[side:]
    probe_f32[...] = probe[...].astype(jnp.float32)
    inten[...] = inten_in[...]
    for target, first, second in ((plain, -sin_part, sin_part), (turned, sin_part, -sin_part)):
        target[:side, :side] = cos_part
        target[side:, side:] = cos_part
        target[:side, side:] = first
        target[side:, :side] = second


def prepare(probe, inten):
    side = probe.shape[1]
    table = jnp.asarray(dft_tables(side))
    square = jax.ShapeDtypeStruct((2 * side, 2 * side), table.dtype)
    return small_kernel(
        prepare_kernel,
        [shape(*probe.shape), jax.ShapeDtypeStruct(inten.shape, inten.dtype), square, square],
        probe,
        inten,
        table,
        name="prepare",
    )


def point_sums(place, counts, spots, own, halos, prepared, owners):
    probe, inten, plain, turned = prepared
    side = probe.shape[1]
    blocks = own.shape[2] // LANES
    rows = own.shape[1] + side
    width = blocks // owners

    def piece(count):
        return jax.ShapeDtypeStruct((count, 2, rows, LANES), jnp.float32)

    mode_sum = jax.ShapeDtypeStruct((side, 2 * side), jnp.float32)
    smem = pl.BlockSpec(memory_space=pltpu.SMEM)
    vmem = pl.BlockSpec(memory_space=pltpu.VMEM)
    anywhere = pl.BlockSpec(memory_space=pl.ANY)
    slots = inten.shape[0]
    return pl.pallas_call(
        functools.partial(point_kernel, owners=owners),
        out_shape=[piece(width)] * 2 + [piece(blocks // 2 - width)] * 2 + [mode_sum] * 2,
        in_specs=[smem] * 3 + [anywhere] * 5 + [vmem] * 4,
        out_specs=[anywhere] * 6,
        scratch_shapes=[
            pltpu.VMEM((2, blocks + 1, rows, LANES), jnp.float32),
            pltpu.VMEM((blocks + 1, 2, rows, LANES), jnp.float32),
            pltpu.VMEM((2, side, 2 * side), jnp.float32),
            *[pltpu.VMEM((2, side, side), jnp.float32)] * 2,
            *[pltpu.VMEM((2 * side, 2 * side), jnp.bfloat16)] * 4,
            *[pltpu.VMEM((2 * side, 2 * side), jnp.float32)] * 2,
            pltpu.SemaphoreType.DMA((6 * blocks,)),
            pltpu.SemaphoreType.DMA((owners + 2,)),
        ],
        compiler_params=pltpu.CompilerParams(vmem_limit_bytes=24 * 1024 * 1024),
        cost_estimate=pl.CostEstimate(
            flops=slots * 32 * 2 * side**3, bytes_accessed=16 * 1024 * 1024, transcendentals=0
        ),
        name="point_sums",
    )(place, counts, spots, own, *halos, *prepared)


def with_neighbours(first, second, turns=(0, 1)):
    count = lax.axis_size("tiles")
    pairs = [(i, i + 1) for i in range(count - 1)]
    return [
        lax.ppermute(cells, "tiles", [x for a, b in pairs[turn::2] for x in ((a, b), (b, a))])
        for turn, cells in zip(turns, (first, second))
    ]


def swap(cells):
    return lax.ppermute(cells, "modes", [(0, 1), (1, 0)])


def rotated(cells, axis, step):
    count = lax.axis_size(axis)
    return lax.ppermute(cells, axis, [(i, (i + step) % count) for i in range(count)])


def small_kernel(body, out_shape, *args, name):
    return pl.pallas_call(
        body,
        out_shape=out_shape,
        in_specs=[
            pl.BlockSpec(memory_space=pltpu.SMEM if x.dtype == jnp.int32 else pltpu.VMEM)
            for x in args
        ],
        out_specs=jax.tree.map(lambda _: pl.BlockSpec(memory_space=pltpu.VMEM), out_shape),
        compiler_params=pltpu.CompilerParams(vmem_limit_bytes=4 * 1024 * 1024),
        cost_estimate=pl.CostEstimate(flops=0, bytes_accessed=0, transcendentals=0),
        name=name,
    )(*args)


def shape(*dims):
    return jax.ShapeDtypeStruct(dims, jnp.float32)


def after(cells, *earlier):
    return lax.optimization_barrier((cells, *earlier))[0]


def add_kernel(*refs):
    total = refs[0][...]
    for ref in refs[1:-1]:
        total = total + ref[...]
    refs[-1][...] = total


def others_kernel(kept, got, *outs):
    width, _, rows = outs[1].shape[:3]
    rim = outs[0].shape[2] // 2
    for step in range(len(outs) // 2):
        rims, core = outs[2 * step : 2 * step + 2]
        cut = slice(step * width, (step + 1) * width)
        rims[:, :, :rim] = kept[cut, :, :rim] + got[cut, :, :rim]
        rims[:, :, rim:] = kept[cut, :, rim + rows :] + got[cut, :, rim + rows :]
        core[...] = kept[cut, :, rim : rim + rows] + got[cut, :, rim : rim + rows]


def mine_kernel(place, kept, got, *rest):
    first, core, second = rest[-3:]
    rim, rows = first.shape[2], core.shape[2]
    total_above = kept[:, :, :rim] + got[:, :, :rim]
    total_below = kept[:, :, rim + rows :] + got[:, :, rim + rows :]
    for other in rest[:-3]:
        total_above = total_above + other[:, :, :rim]
        total_below = total_below + other[:, :, rim:]
    even = place[0] % 2 == 0

    @pl.when(even)
    def below_first():
        first[...] = total_below
        second[...] = total_above

    @pl.when(~even)
    def above_first():
        first[...] = total_above
        second[...] = total_below

    core[...] = kept[:, :, rim : rim + rows] + got[:, :, rim : rim + rows]


def fold_kernel(place, core, second, first, out):
    rim, rows = first.shape[2], core.shape[2]
    out[...] = core[...]
    near = pl.multiple_of((place[0] % 2) * (rows - rim), 8)
    far = pl.multiple_of(rows - rim - near, 8)
    out[:, :, pl.ds(far, rim)] += first[...]
    out[:, :, pl.ds(near, rim)] += second[...]


def finish_kernel(core, *rest):
    out = rest[-1]
    for block in range(core.shape[0]):
        total = core[block]
        for other in rest[:-1]:
            total = total + other[block]
        out[:, :, block * LANES : (block + 1) * LANES] = total


def share_rows(index, share):
    return pl.ds(pl.multiple_of(index * share, share), share)


def shares_kernel(place, kept, got, *outs):
    share = outs[0].shape[0]
    for step, out in enumerate(outs):
        rows = share_rows(place[0] ^ step, share)
        out[...] = kept[rows] + got[rows]


def gather_kernel(place, *refs):
    out, sems = refs[-2:]
    parts = refs[:-2]
    tiles = len(parts) // 2
    share = parts[0].shape[0]
    copies = []
    for index, part in enumerate(parts):
        swapped, step = divmod(index, tiles)
        mode = place[2] if swapped == 0 else 1 - place[2]
        target = out.at[mode, share_rows(place[0] ^ step, share)]
        copies.append(pltpu.make_async_copy(part, target, sems.at[index]))
    for copy in copies:
        copy.start()
    for copy in copies:
        copy.wait()


def gather_parts(place, parts):
    tiles = len(parts) // 2
    share, width = parts[0].shape
    return pl.pallas_call(
        gather_kernel,
        out_shape=shape(2, tiles * share, width),
        in_specs=[pl.BlockSpec(memory_space=pltpu.SMEM)]
        + [pl.BlockSpec(memory_space=pltpu.VMEM)] * len(parts),
        out_specs=pl.BlockSpec(memory_space=pl.ANY),
        scratch_shapes=[pltpu.SemaphoreType.DMA((len(parts),))],
        compiler_params=pltpu.CompilerParams(vmem_limit_bytes=4 * 1024 * 1024),
        name="probe_gather",
    )(place, *parts)


def on_device(object_field, probe, intensity, centres, counts):
    side = probe.shape[1]
    rim = side // 2
    strip_rows, cols = object_field.shape[1:]
    strip = lax.axis_index("tiles")
    sub = lax.axis_index("sub")
    mode = lax.axis_index("modes")
    tiles, subs = lax.axis_size("tiles"), lax.axis_size("sub")
    owners = subs * lax.axis_size("modes")
    width = cols // owners // LANES
    place = jnp.stack([strip, sub, mode]).astype(jnp.int32)

    last = strip_rows - rim
    even = strip % 2 == 0
    ends = [
        lax.dynamic_slice(object_field, (mode, jnp.where(at_end, last, 0), 0), (1, rim, cols))[0]
        for at_end in (even, ~even)
    ]
    first, second = with_neighbours(*ends)
    halos = (first, second, swap(first), swap(second))

    keep_mine, give_mine, keep_others, give_others, keep_probe, give_probe = point_sums(
        place, counts, centres.reshape(-1), object_field, halos, prepare(probe, intensity[0]), owners
    )
    got_probe = swap(give_probe)
    got_others = swap(give_others)
    got_mine = swap(give_mine)

    rims_shape = shape(width, 2, 2 * rim, LANES)
    core_shape = shape(width, 2, strip_rows, LANES)
    direct = tiles in (1, 2, 4)
    total_rows, total_cols = keep_probe.shape
    share = shape(total_rows // tiles, total_cols)
    if direct:
        parts = small_kernel(
            shares_kernel, [share] * tiles, place, keep_probe, got_probe, name="probe_shares"
        )
        got_others, *parts = lax.optimization_barrier((got_others, *parts))
    outgoing = list(small_kernel(
        others_kernel,
        [rims_shape, core_shape] * (subs - 1),
        keep_others,
        got_others,
        name="object_others",
    ))

    def rotate_all(parts):
        return [rotated(x, "sub", step + 1) for step, x in enumerate(parts)]

    def rotate_strips(parts):
        return [
            lax.ppermute(x, "tiles", [(i, i ^ (step + 1)) for i in range(tiles)])
            for step, x in enumerate(parts)
        ]

    if direct:
        parts_in = rotate_strips(parts[1:])
    rims_in = rotate_all(outgoing[0::2])
    core_out = outgoing[1::2]
    first, core, second = small_kernel(
        mine_kernel,
        [shape(width, 2, rim, LANES), core_shape, shape(width, 2, rim, LANES)],
        place,
        keep_mine,
        got_mine,
        *rims_in,
        name="object_mine",
    )
    if direct:
        part_sum = small_kernel(add_kernel, share, parts[0], *parts_in, name="probe_strips_sum")
        part_sum, first, second = lax.optimization_barrier((part_sum, first, second))
        part_in = [rotated(part_sum, "sub", step) for step in range(1, subs)]
    second, first = with_neighbours(second, first, (1, 0))
    if direct:
        part_sum = small_kernel(add_kernel, share, part_sum, *part_in, name="probe_total")
        part_sum, core, *core_out = lax.optimization_barrier((part_sum, core, *core_out))
        parts_in = rotate_strips([part_sum] * (tiles - 1))
    folded = small_kernel(
        fold_kernel, core_shape, place, core, second, first, name="object_fold"
    )
    if direct:
        parts_in[1], folded = lax.optimization_barrier((parts_in[1], folded))
    core_in = rotate_all(core_out)
    object_grad = small_kernel(
        finish_kernel,
        shape(2, strip_rows, width * LANES),
        folded,
        *core_in,
        name="object_finish",
    )
    if direct:
        parts = [part_sum, *parts_in]
    else:
        parts = [lax.psum(keep_probe + got_probe, ("tiles", "sub"))]
    spot = place if direct else place * jnp.array([0, 0, 1], jnp.int32)
    probe_grad = gather_parts(spot, [*parts, *[swap(x) for x in parts]])
    return (object_grad, probe_grad)


def solution(mesh):
    return jax.shard_map(
        on_device,
        mesh=mesh,
        in_specs=(
            P(None, ("groups", "tiles"), None),
            P("groups", None, None),
            P(("groups", "tiles"), ("sub", "modes"), None, None),
            P(("groups", "tiles"), None, None),
            P(("groups", "tiles")),
        ),
        out_specs=(P(None, ("groups", "tiles"), ("sub", "modes")), P("groups", None, None)),
        check_vma=False,
    )
```

```python
import functools
import math

import jax
import jax.numpy as jnp
import ml_dtypes
import numpy as np
from jax import lax
from jax.experimental import pallas as pl
from jax.experimental.pallas import tpu as pltpu
from jax.sharding import PartitionSpec as P

LANES = 128
CHUNK = 16


def dft_tables(size):
    index = np.arange(size)
    angle = (index[:, None] * index[None, :] % size) * (2.0 * math.pi / size)
    scale = 1.0 / math.sqrt(size)
    cos_part = (np.cos(angle) * scale).astype(np.float32).astype(ml_dtypes.bfloat16)
    sin_part = (-np.sin(angle) * scale).astype(np.float32).astype(ml_dtypes.bfloat16)
    return np.concatenate([cos_part, sin_part])


def interleave(first, second):
    done = 0
    for index, step in enumerate(first):
        step()
        upto = (index + 1) * len(second) // len(first)
        for other in second[done:upto]:
            other()
        done = upto


def point_kernel(
    place,
    counts,
    spots,
    own,
    first_a,
    second_a,
    first_b,
    second_b,
    probe_f32,
    inten,
    plain,
    turned,
    *rest,
    owners,
):
    keep_mine, give_mine, keep_others, give_others, keep_probe, give_probe = rest[:6]
    field, grad, probe_grad = rest[6:9]
    patches, waves, halves, fars = (rest[9 + 2 * i : 11 + 2 * i] for i in range(4))
    sems, out_sems = rest[17:]
    strip, sub, mode = place[0], place[1], place[2]
    member = sub * 2 + mode
    side = probe_f32.shape[1]
    rim = side // 2
    strip_rows = own.shape[1]
    blocks = own.shape[2] // LANES
    slots = inten.shape[0]
    total = jnp.clip(counts[0] - member * slots, 0, slots)
    far_rows = rim + strip_rows
    near = (strip % 2) * far_rows
    copies = []

    def fetch(src, dst):
        copies.append(pltpu.make_async_copy(src, dst, sems.at[len(copies)]))

    for block in range(blocks):
        cols = pl.ds(block * LANES, LANES)
        for plane in range(2):
            fetch(own.at[plane, :, cols], field.at[plane, block, pl.ds(rim, strip_rows)])
        for first, second, plane in ((first_a, second_a, mode), (first_b, second_b, 1 - mode)):
            fetch(first.at[:, cols], field.at[plane, block, pl.ds(far_rows - near, rim)])
            fetch(second.at[:, cols], field.at[plane, block, pl.ds(near, rim)])
    for copy in copies:
        copy.start()

    probe_grad[...] = jnp.zeros_like(probe_grad)
    patches[1][...] = jnp.zeros_like(patches[1])
    fars[1][...] = jnp.zeros_like(fars[1])

    @pl.loop(0, grad.shape[0])
    def clear(block):
        grad[block] = jnp.zeros(grad.shape[1:], jnp.float32)

    for copy in copies:
        copy.wait()

    lane = lax.broadcasted_iota(jnp.int32, (CHUNK, LANES), 1)
    chunks = range(0, side, CHUNK)

    def spot(slot):
        base = 2 * (member * slots + jnp.clip(slot, 0, slots - 1))
        row = spots[base] - strip * strip_rows
        col = spots[base + 1] - rim
        return row, col // LANES, col % LANES

    def cut(k, slot):
        row, block, off = spot(slot)
        back_shift = (LANES - off) % LANES
        patch, wave = patches[k], waves[k]

        def step(chunk):
            rows = slice(chunk, chunk + CHUNK)
            low = slice(side + chunk, side + chunk + CHUNK)
            source = pl.ds(row + chunk, CHUNK)
            obj = []
            for plane in range(2):
                rolled = [
                    pltpu.roll(field[plane, block + j, source, :], back_shift, 1)
                    for j in range(3)
                ]
                obj.append(
                    [jnp.where(lane < LANES - off, rolled[j], rolled[j + 1]) for j in range(2)]
                )
            for j in range(2):
                cols = slice(j * LANES, (j + 1) * LANES)
                obj_re, obj_im = obj[0][j], obj[1][j]
                patch[0, rows, cols] = obj_re
                patch[1, rows, cols] = obj_im
                for m in range(2):
                    probe_re = probe_f32[m, rows, cols]
                    probe_im = probe_f32[m, rows, side + j * LANES : side + (j + 1) * LANES]
                    out = slice(m * side + j * LANES, m * side + (j + 1) * LANES)
                    wave[rows, out] = (probe_re * obj_re - probe_im * obj_im).astype(jnp.bfloat16)
                    wave[low, out] = (probe_re * obj_im + probe_im * obj_re).astype(jnp.bfloat16)

        return [functools.partial(step, chunk) for chunk in chunks]

    def left(k, table):
        wave, half = waves[k], halves[k]

        def step(m):
            cols = slice(m * side, (m + 1) * side)
            stacked = jnp.dot(table[...], wave[:, cols], preferred_element_type=jnp.float32)
            half[cols, :side] = stacked[:side].astype(jnp.bfloat16)
            half[cols, side:] = stacked[side:].astype(jnp.bfloat16)

        return [functools.partial(step, m) for m in range(2)]

    def right(k, table):
        half, far = halves[k], fars[k]

        def step(m):
            rows = slice(m * side, (m + 1) * side)
            far[rows] = jnp.dot(half[rows], table[...], preferred_element_type=jnp.float32)

        return [functools.partial(step, m) for m in range(2)]

    def compare(k, slot):
        far, wave = fars[k], waves[k]
        valid = jnp.where(slot < total, 1.0, 0.0)

        def step(chunk):
            parts = []
            power = 1.0
            for m in range(2):
                rows = slice(m * side + chunk, m * side + chunk + CHUNK)
                far_re, far_im = far[rows, :side], far[rows, side:]
                power = power + (far_re * far_re + far_im * far_im)
                parts.append((far_re, far_im))
            level = inten[jnp.clip(slot, 0, slots - 1), chunk : chunk + CHUNK]
            level = level.astype(jnp.float32) + 1.0
            ratio = valid - (valid * level) * lax.rsqrt(level * power)
            for m in range(2):
                cols = slice(m * side, (m + 1) * side)
                wave[chunk : chunk + CHUNK, cols] = (parts[m][0] * ratio).astype(jnp.bfloat16)
                wave[side + chunk : side + chunk + CHUNK, cols] = (parts[m][1] * ratio).astype(
                    jnp.bfloat16
                )

        return [functools.partial(step, chunk) for chunk in chunks]

    def gather(k, slot):
        row, block, off = spot(slot)
        far, patch = fars[k], patches[k]

        def step(chunk):
            rows = slice(chunk, chunk + CHUNK)
            obj_re, obj_im = patch[0, rows], patch[1, rows]
            terms = [0.0, 0.0]
            for m in range(2):
                probe_re = probe_f32[m, rows, :side]
                probe_im = probe_f32[m, rows, side:]
                far_rows = slice(m * side + chunk, m * side + chunk + CHUNK)
                back_re, back_im = far[far_rows, :side], far[far_rows, side:]
                terms[0] = terms[0] + (probe_re * back_re + probe_im * back_im)
                terms[1] = terms[1] + (probe_re * back_im - probe_im * back_re)
                probe_grad[m, rows, :side] += obj_re * back_re + obj_im * back_im
                probe_grad[m, rows, side:] += obj_re * back_im - obj_im * back_re
            target = pl.ds(row + chunk, CHUNK)
            for plane in range(2):
                first = pltpu.roll(terms[plane][:, :LANES], off, 1)
                second = pltpu.roll(terms[plane][:, LANES:], off, 1)
                grad[block, plane, target, :] += jnp.where(lane < off, 0.0, first)
                grad[block + 1, plane, target, :] += jnp.where(lane < off, first, second)
                grad[block + 2, plane, target, :] += jnp.where(lane < off, second, 0.0)

        return [functools.partial(step, chunk) for chunk in chunks]

    for step in cut(0, 0):
        step()

    @pl.loop(0, (total + 1) // 2)
    def pair(index):
        slot = 2 * index
        interleave(left(0, plain) + right(0, turned), gather(1, slot - 1) + cut(1, slot + 1))
        interleave(left(1, plain) + right(1, turned), compare(0, slot))
        interleave(left(0, turned) + right(0, plain), compare(1, slot + 1))
        interleave(left(1, turned) + right(1, plain), gather(0, slot) + cut(0, slot + 2))

    for step in gather(1, 2 * ((total + 1) // 2) - 1):
        step()

    width = blocks // owners
    sends = []

    def send(src, dst):
        sends.append(pltpu.make_async_copy(src, dst, out_sems.at[len(sends)]))

    send(probe_grad.at[1 - mode], give_probe)
    send(probe_grad.at[mode], keep_probe)
    for step in list(range(1, owners // 2)) + [0]:
        owner = 2 * lax.rem(sub + step, owners // 2)
        for part, target in (
            (owner + 1 - mode, give_others if step else give_mine),
            (owner + mode, keep_others if step else keep_mine),
        ):
            if step:
                target = target.at[pl.ds((step - 1) * width, width)]
            send(grad.at[pl.ds(part * width, width)], target)
    for copy in sends:
        copy.start()
    for copy in sends:
        copy.wait()


def prepare_kernel(probe, inten_in, table, probe_f32, inten, plain, turned):
    side = table.shape[1]
    cos_part, sin_part = table[:side], table[side:]
    probe_f32[...] = probe[...].astype(jnp.float32)
    inten[...] = inten_in[...]
    for target, first, second in ((plain, -sin_part, sin_part), (turned, sin_part, -sin_part)):
        target[:side, :side] = cos_part
        target[side:, side:] = cos_part
        target[:side, side:] = first
        target[side:, :side] = second


def prepare(probe, inten):
    side = probe.shape[1]
    table = jnp.asarray(dft_tables(side))
    square = jax.ShapeDtypeStruct((2 * side, 2 * side), table.dtype)
    return small_kernel(
        prepare_kernel,
        [shape(*probe.shape), jax.ShapeDtypeStruct(inten.shape, inten.dtype), square, square],
        probe,
        inten,
        table,
        name="prepare",
    )


def point_sums(place, counts, spots, own, halos, prepared, owners):
    probe, inten, plain, turned = prepared
    side = probe.shape[1]
    blocks = own.shape[2] // LANES
    rows = own.shape[1] + side
    width = blocks // owners

    def piece(count):
        return jax.ShapeDtypeStruct((count, 2, rows, LANES), jnp.float32)

    mode_sum = jax.ShapeDtypeStruct((side, 2 * side), jnp.float32)
    smem = pl.BlockSpec(memory_space=pltpu.SMEM)
    vmem = pl.BlockSpec(memory_space=pltpu.VMEM)
    anywhere = pl.BlockSpec(memory_space=pl.ANY)
    slots = inten.shape[0]
    return pl.pallas_call(
        functools.partial(point_kernel, owners=owners),
        out_shape=[piece(width)] * 2 + [piece(blocks // 2 - width)] * 2 + [mode_sum] * 2,
        in_specs=[smem] * 3 + [anywhere] * 5 + [vmem] * 4,
        out_specs=[anywhere] * 6,
        scratch_shapes=[
            pltpu.VMEM((2, blocks + 1, rows, LANES), jnp.float32),
            pltpu.VMEM((blocks + 1, 2, rows, LANES), jnp.float32),
            pltpu.VMEM((2, side, 2 * side), jnp.float32),
            *[pltpu.VMEM((2, side, side), jnp.float32)] * 2,
            *[pltpu.VMEM((2 * side, 2 * side), jnp.bfloat16)] * 4,
            *[pltpu.VMEM((2 * side, 2 * side), jnp.float32)] * 2,
            pltpu.SemaphoreType.DMA((6 * blocks,)),
            pltpu.SemaphoreType.DMA((owners + 2,)),
        ],
        compiler_params=pltpu.CompilerParams(vmem_limit_bytes=24 * 1024 * 1024),
        cost_estimate=pl.CostEstimate(
            flops=slots * 32 * 2 * side**3, bytes_accessed=16 * 1024 * 1024, transcendentals=0
        ),
        name="point_sums",
    )(place, counts, spots, own, *halos, *prepared)


def with_neighbours(first, second, turns=(0, 1)):
    count = lax.axis_size("tiles")
    pairs = [(i, i + 1) for i in range(count - 1)]
    return [
        lax.ppermute(cells, "tiles", [x for a, b in pairs[turn::2] for x in ((a, b), (b, a))])
        for turn, cells in zip(turns, (first, second))
    ]


def swap(cells):
    return lax.ppermute(cells, "modes", [(0, 1), (1, 0)])


def rotated(cells, axis, step):
    count = lax.axis_size(axis)
    return lax.ppermute(cells, axis, [(i, (i + step) % count) for i in range(count)])


def small_kernel(body, out_shape, *args, name):
    return pl.pallas_call(
        body,
        out_shape=out_shape,
        in_specs=[
            pl.BlockSpec(memory_space=pltpu.SMEM if x.dtype == jnp.int32 else pltpu.VMEM)
            for x in args
        ],
        out_specs=jax.tree.map(lambda _: pl.BlockSpec(memory_space=pltpu.VMEM), out_shape),
        compiler_params=pltpu.CompilerParams(vmem_limit_bytes=4 * 1024 * 1024),
        cost_estimate=pl.CostEstimate(flops=0, bytes_accessed=0, transcendentals=0),
        name=name,
    )(*args)


def shape(*dims):
    return jax.ShapeDtypeStruct(dims, jnp.float32)


def after(cells, *earlier):
    return lax.optimization_barrier((cells, *earlier))[0]


def add_kernel(*refs):
    total = refs[0][...]
    for ref in refs[1:-1]:
        total = total + ref[...]
    refs[-1][...] = total


def others_kernel(kept, got, *outs):
    width, _, rows = outs[1].shape[:3]
    rim = outs[0].shape[2] // 2
    for step in range(len(outs) // 2):
        rims, core = outs[2 * step : 2 * step + 2]
        cut = slice(step * width, (step + 1) * width)
        rims[:, :, :rim] = kept[cut, :, :rim] + got[cut, :, :rim]
        rims[:, :, rim:] = kept[cut, :, rim + rows :] + got[cut, :, rim + rows :]
        core[...] = kept[cut, :, rim : rim + rows] + got[cut, :, rim : rim + rows]


def mine_kernel(place, kept, got, *rest):
    first, core, second = rest[-3:]
    rim, rows = first.shape[2], core.shape[2]
    total_above = kept[:, :, :rim] + got[:, :, :rim]
    total_below = kept[:, :, rim + rows :] + got[:, :, rim + rows :]
    for other in rest[:-3]:
        total_above = total_above + other[:, :, :rim]
        total_below = total_below + other[:, :, rim:]
    even = place[0] % 2 == 0

    @pl.when(even)
    def below_first():
        first[...] = total_below
        second[...] = total_above

    @pl.when(~even)
    def above_first():
        first[...] = total_above
        second[...] = total_below

    core[...] = kept[:, :, rim : rim + rows] + got[:, :, rim : rim + rows]


def fold_kernel(place, core, second, first, out):
    rim, rows = first.shape[2], core.shape[2]
    out[...] = core[...]
    near = pl.multiple_of((place[0] % 2) * (rows - rim), 8)
    far = pl.multiple_of(rows - rim - near, 8)
    out[:, :, pl.ds(far, rim)] += first[...]
    out[:, :, pl.ds(near, rim)] += second[...]


def finish_kernel(core, *rest):
    out = rest[-1]
    for block in range(core.shape[0]):
        total = core[block]
        for other in rest[:-1]:
            total = total + other[block]
        out[:, :, block * LANES : (block + 1) * LANES] = total


def share_rows(index, share):
    return pl.ds(pl.multiple_of(index * share, share), share)


def shares_kernel(place, kept, got, *outs):
    share = outs[0].shape[0]
    for step, out in enumerate(outs):
        rows = share_rows(place[0] ^ step, share)
        out[...] = kept[rows] + got[rows]


def gather_kernel(place, *refs):
    out, sems = refs[-2:]
    parts = refs[:-2]
    tiles = len(parts) // 2
    share = parts[0].shape[0]
    copies = []
    for index, part in enumerate(parts):
        swapped, step = divmod(index, tiles)
        mode = place[2] if swapped == 0 else 1 - place[2]
        target = out.at[mode, share_rows(place[0] ^ step, share)]
        copies.append(pltpu.make_async_copy(part, target, sems.at[index]))
    for copy in copies:
        copy.start()
    for copy in copies:
        copy.wait()


def gather_parts(place, parts):
    tiles = len(parts) // 2
    share, width = parts[0].shape
    return pl.pallas_call(
        gather_kernel,
        out_shape=shape(2, tiles * share, width),
        in_specs=[pl.BlockSpec(memory_space=pltpu.SMEM)]
        + [pl.BlockSpec(memory_space=pltpu.VMEM)] * len(parts),
        out_specs=pl.BlockSpec(memory_space=pl.ANY),
        scratch_shapes=[pltpu.SemaphoreType.DMA((len(parts),))],
        compiler_params=pltpu.CompilerParams(vmem_limit_bytes=4 * 1024 * 1024),
        name="probe_gather",
    )(place, *parts)


def on_device(object_field, probe, intensity, centres, counts):
    side = probe.shape[1]
    rim = side // 2
    strip_rows, cols = object_field.shape[1:]
    strip = lax.axis_index("tiles")
    sub = lax.axis_index("sub")
    mode = lax.axis_index("modes")
    tiles, subs = lax.axis_size("tiles"), lax.axis_size("sub")
    owners = subs * lax.axis_size("modes")
    width = cols // owners // LANES
    place = jnp.stack([strip, sub, mode]).astype(jnp.int32)

    last = strip_rows - rim
    even = strip % 2 == 0
    ends = [
        lax.dynamic_slice(object_field, (mode, jnp.where(at_end, last, 0), 0), (1, rim, cols))[0]
        for at_end in (even, ~even)
    ]
    first, second = with_neighbours(*ends)
    halos = (first, second, swap(first), swap(second))

    keep_mine, give_mine, keep_others, give_others, keep_probe, give_probe = point_sums(
        place, counts, centres.reshape(-1), object_field, halos, prepare(probe, intensity[0]), owners
    )
    got_probe = swap(give_probe)
    got_others = swap(give_others)
    got_mine = swap(give_mine)

    rims_shape = shape(width, 2, 2 * rim, LANES)
    core_shape = shape(width, 2, strip_rows, LANES)
    direct = tiles in (1, 2, 4)
    total_rows, total_cols = keep_probe.shape
    share = shape(total_rows // tiles, total_cols)
    if direct:
        parts = small_kernel(
            shares_kernel, [share] * tiles, place, keep_probe, got_probe, name="probe_shares"
        )
        got_others, *parts = lax.optimization_barrier((got_others, *parts))
    outgoing = list(small_kernel(
        others_kernel,
        [rims_shape, core_shape] * (subs - 1),
        keep_others,
        got_others,
        name="object_others",
    ))

    def rotate_all(parts):
        return [rotated(x, "sub", step + 1) for step, x in enumerate(parts)]

    def rotate_strips(parts):
        return [
            lax.ppermute(x, "tiles", [(i, i ^ (step + 1)) for i in range(tiles)])
            for step, x in enumerate(parts)
        ]

    if direct:
        parts_in = rotate_strips(parts[1:])
    rims_in = rotate_all(outgoing[0::2])
    core_out = outgoing[1::2]
    first, core, second = small_kernel(
        mine_kernel,
        [shape(width, 2, rim, LANES), core_shape, shape(width, 2, rim, LANES)],
        place,
        keep_mine,
        got_mine,
        *rims_in,
        name="object_mine",
    )
    if direct:
        part_sum = small_kernel(add_kernel, share, parts[0], *parts_in, name="probe_strips_sum")
        part_sum, first, second = lax.optimization_barrier((part_sum, first, second))
        part_in = [rotated(part_sum, "sub", step) for step in range(1, subs)]
    second, first = with_neighbours(second, first, (1, 0))
    if direct:
        part_sum = small_kernel(add_kernel, share, part_sum, *part_in, name="probe_total")
        part_sum, core, *core_out = lax.optimization_barrier((part_sum, core, *core_out))
        parts_in = rotate_strips([part_sum] * (tiles - 1))
    folded = small_kernel(
        fold_kernel, core_shape, place, core, second, first, name="object_fold"
    )
    if direct:
        parts_in[1], folded = lax.optimization_barrier((parts_in[1], folded))
    core_in = rotate_all(core_out)
    object_grad = small_kernel(
        finish_kernel,
        shape(2, strip_rows, width * LANES),
        folded,
        *core_in,
        name="object_finish",
    )
    if direct:
        parts = [part_sum, *parts_in]
    else:
        parts = [lax.psum(keep_probe + got_probe, ("tiles", "sub"))]
    spot = place if direct else place * jnp.array([0, 0, 1], jnp.int32)
    probe_grad = gather_parts(spot, [*parts, *[swap(x) for x in parts]])
    return (object_grad, probe_grad)


def solution(mesh):
    return jax.shard_map(
        on_device,
        mesh=mesh,
        in_specs=(
            P(None, ("groups", "tiles"), None),
            P("groups", None, None),
            P(("groups", "tiles"), ("sub", "modes"), None, None),
            P(("groups", "tiles"), None, None),
            P(("groups", "tiles")),
        ),
        out_specs=(P(None, ("groups", "tiles"), ("sub", "modes")), P("groups", None, None)),
        check_vma=False,
    )
```

```python
import functools
import math

import jax
import jax.numpy as jnp
import ml_dtypes
import numpy as np
from jax import lax
from jax.experimental import pallas as pl
from jax.experimental.pallas import tpu as pltpu
from jax.sharding import PartitionSpec as P

LANES = 128
CHUNK = 16


def dft_tables(size):
    index = np.arange(size)
    angle = (index[:, None] * index[None, :] % size) * (2.0 * math.pi / size)
    scale = 1.0 / math.sqrt(size)
    cos_part = (np.cos(angle) * scale).astype(np.float32).astype(ml_dtypes.bfloat16)
    sin_part = (-np.sin(angle) * scale).astype(np.float32).astype(ml_dtypes.bfloat16)
    return np.concatenate([cos_part, sin_part])


def interleave(first, second):
    done = 0
    for index, step in enumerate(first):
        step()
        upto = (index + 1) * len(second) // len(first)
        for other in second[done:upto]:
            other()
        done = upto


def point_kernel(
    place,
    counts,
    spots,
    own,
    first_a,
    second_a,
    first_b,
    second_b,
    probe_f32,
    inten,
    plain,
    turned,
    *rest,
    owners,
):
    keep_mine, give_mine, keep_others, give_others, keep_probe, give_probe = rest[:6]
    field, grad, probe_grad = rest[6:9]
    patches, waves, halves, fars = (rest[9 + 2 * i : 11 + 2 * i] for i in range(4))
    sems, out_sems = rest[17:]
    strip, sub, mode = place[0], place[1], place[2]
    member = sub * 2 + mode
    side = probe_f32.shape[1]
    rim = side // 2
    strip_rows = own.shape[1]
    blocks = own.shape[2] // LANES
    slots = inten.shape[0]
    total = jnp.clip(counts[0] - member * slots, 0, slots)
    far_rows = rim + strip_rows
    near = (strip % 2) * far_rows
    copies = []

    def fetch(src, dst):
        copies.append(pltpu.make_async_copy(src, dst, sems.at[len(copies)]))

    for block in range(blocks):
        cols = pl.ds(block * LANES, LANES)
        for plane in range(2):
            fetch(own.at[plane, :, cols], field.at[plane, block, pl.ds(rim, strip_rows)])
        for first, second, plane in ((first_a, second_a, mode), (first_b, second_b, 1 - mode)):
            fetch(first.at[:, cols], field.at[plane, block, pl.ds(far_rows - near, rim)])
            fetch(second.at[:, cols], field.at[plane, block, pl.ds(near, rim)])
    for copy in copies:
        copy.start()

    probe_grad[...] = jnp.zeros_like(probe_grad)
    patches[1][...] = jnp.zeros_like(patches[1])
    fars[1][...] = jnp.zeros_like(fars[1])

    @pl.loop(0, grad.shape[0])
    def clear(block):
        grad[block] = jnp.zeros(grad.shape[1:], jnp.float32)

    for copy in copies:
        copy.wait()

    lane = lax.broadcasted_iota(jnp.int32, (CHUNK, LANES), 1)
    chunks = range(0, side, CHUNK)

    def spot(slot):
        base = 2 * (member * slots + jnp.clip(slot, 0, slots - 1))
        row = spots[base] - strip * strip_rows
        col = spots[base + 1] - rim
        return row, col // LANES, col % LANES

    def cut(k, slot):
        row, block, off = spot(slot)
        back_shift = (LANES - off) % LANES
        patch, wave = patches[k], waves[k]

        def step(chunk):
            rows = slice(chunk, chunk + CHUNK)
            low = slice(side + chunk, side + chunk + CHUNK)
            source = pl.ds(row + chunk, CHUNK)
            obj = []
            for plane in range(2):
                rolled = [
                    pltpu.roll(field[plane, block + j, source, :], back_shift, 1)
                    for j in range(3)
                ]
                obj.append(
                    [jnp.where(lane < LANES - off, rolled[j], rolled[j + 1]) for j in range(2)]
                )
            for j in range(2):
                cols = slice(j * LANES, (j + 1) * LANES)
                obj_re, obj_im = obj[0][j], obj[1][j]
                patch[0, rows, cols] = obj_re
                patch[1, rows, cols] = obj_im
                for m in range(2):
                    probe_re = probe_f32[m, rows, cols]
                    probe_im = probe_f32[m, rows, side + j * LANES : side + (j + 1) * LANES]
                    out = slice(m * side + j * LANES, m * side + (j + 1) * LANES)
                    wave[rows, out] = (probe_re * obj_re - probe_im * obj_im).astype(jnp.bfloat16)
                    wave[low, out] = (probe_re * obj_im + probe_im * obj_re).astype(jnp.bfloat16)

        return [functools.partial(step, chunk) for chunk in chunks]

    def left(k, table):
        wave, half = waves[k], halves[k]

        def step(m):
            cols = slice(m * side, (m + 1) * side)
            stacked = jnp.dot(table[...], wave[:, cols], preferred_element_type=jnp.float32)
            half[cols, :side] = stacked[:side].astype(jnp.bfloat16)
            half[cols, side:] = stacked[side:].astype(jnp.bfloat16)

        return [functools.partial(step, m) for m in range(2)]

    def right(k, table):
        half, far = halves[k], fars[k]

        def step(m):
            rows = slice(m * side, (m + 1) * side)
            far[rows] = jnp.dot(half[rows], table[...], preferred_element_type=jnp.float32)

        return [functools.partial(step, m) for m in range(2)]

    def compare(k, slot):
        far, wave = fars[k], waves[k]
        valid = jnp.where(slot < total, 1.0, 0.0)

        def step(chunk):
            parts = []
            power = 1.0
            for m in range(2):
                rows = slice(m * side + chunk, m * side + chunk + CHUNK)
                far_re, far_im = far[rows, :side], far[rows, side:]
                power = power + (far_re * far_re + far_im * far_im)
                parts.append((far_re, far_im))
            level = inten[jnp.clip(slot, 0, slots - 1), chunk : chunk + CHUNK]
            level = level.astype(jnp.float32) + 1.0
            ratio = valid - (valid * level) * lax.rsqrt(level * power)
            for m in range(2):
                cols = slice(m * side, (m + 1) * side)
                wave[chunk : chunk + CHUNK, cols] = (parts[m][0] * ratio).astype(jnp.bfloat16)
                wave[side + chunk : side + chunk + CHUNK, cols] = (parts[m][1] * ratio).astype(
                    jnp.bfloat16
                )

        return [functools.partial(step, chunk) for chunk in chunks]

    def gather(k, slot):
        row, block, off = spot(slot)
        far, patch = fars[k], patches[k]

        def step(chunk):
            rows = slice(chunk, chunk + CHUNK)
            obj_re, obj_im = patch[0, rows], patch[1, rows]
            terms = [0.0, 0.0]
            for m in range(2):
                probe_re = probe_f32[m, rows, :side]
                probe_im = probe_f32[m, rows, side:]
                far_rows = slice(m * side + chunk, m * side + chunk + CHUNK)
                back_re, back_im = far[far_rows, :side], far[far_rows, side:]
                terms[0] = terms[0] + (probe_re * back_re + probe_im * back_im)
                terms[1] = terms[1] + (probe_re * back_im - probe_im * back_re)
                probe_grad[m, rows, :side] += obj_re * back_re + obj_im * back_im
                probe_grad[m, rows, side:] += obj_re * back_im - obj_im * back_re
            target = pl.ds(row + chunk, CHUNK)
            for plane in range(2):
                first = pltpu.roll(terms[plane][:, :LANES], off, 1)
                second = pltpu.roll(terms[plane][:, LANES:], off, 1)
                grad[block, plane, target, :] += jnp.where(lane < off, 0.0, first)
                grad[block + 1, plane, target, :] += jnp.where(lane < off, first, second)
                grad[block + 2, plane, target, :] += jnp.where(lane < off, second, 0.0)

        return [functools.partial(step, chunk) for chunk in chunks]

    for step in cut(0, 0):
        step()

    @pl.loop(0, (total + 1) // 2)
    def pair(index):
        slot = 2 * index
        interleave(left(0, plain) + right(0, turned), gather(1, slot - 1) + cut(1, slot + 1))
        interleave(left(1, plain) + right(1, turned), compare(0, slot))
        interleave(left(0, turned) + right(0, plain), compare(1, slot + 1))
        interleave(left(1, turned) + right(1, plain), gather(0, slot) + cut(0, slot + 2))

    for step in gather(1, 2 * ((total + 1) // 2) - 1):
        step()

    width = blocks // owners
    sends = []

    def send(src, dst):
        sends.append(pltpu.make_async_copy(src, dst, out_sems.at[len(sends)]))

    send(probe_grad.at[1 - mode], give_probe)
    send(probe_grad.at[mode], keep_probe)
    for step in list(range(1, owners // 2)) + [0]:
        owner = 2 * lax.rem(sub + step, owners // 2)
        for part, target in (
            (owner + 1 - mode, give_others if step else give_mine),
            (owner + mode, keep_others if step else keep_mine),
        ):
            if step:
                target = target.at[pl.ds((step - 1) * width, width)]
            send(grad.at[pl.ds(part * width, width)], target)
    for copy in sends:
        copy.start()
    for copy in sends:
        copy.wait()


def prepare_kernel(probe, inten_in, table, probe_f32, inten, plain, turned):
    side = table.shape[1]
    cos_part, sin_part = table[:side], table[side:]
    probe_f32[...] = probe[...].astype(jnp.float32)
    inten[...] = inten_in[...]
    for target, first, second in ((plain, -sin_part, sin_part), (turned, sin_part, -sin_part)):
        target[:side, :side] = cos_part
        target[side:, side:] = cos_part
        target[:side, side:] = first
        target[side:, :side] = second


def prepare(probe, inten):
    side = probe.shape[1]
    table = jnp.asarray(dft_tables(side))
    square = jax.ShapeDtypeStruct((2 * side, 2 * side), table.dtype)
    return small_kernel(
        prepare_kernel,
        [shape(*probe.shape), jax.ShapeDtypeStruct(inten.shape, inten.dtype), square, square],
        probe,
        inten,
        table,
        name="prepare",
    )


def point_sums(place, counts, spots, own, halos, prepared, owners):
    probe, inten, plain, turned = prepared
    side = probe.shape[1]
    blocks = own.shape[2] // LANES
    rows = own.shape[1] + side
    width = blocks // owners

    def piece(count):
        return jax.ShapeDtypeStruct((count, 2, rows, LANES), jnp.float32)

    mode_sum = jax.ShapeDtypeStruct((side, 2 * side), jnp.float32)
    smem = pl.BlockSpec(memory_space=pltpu.SMEM)
    vmem = pl.BlockSpec(memory_space=pltpu.VMEM)
    anywhere = pl.BlockSpec(memory_space=pl.ANY)
    slots = inten.shape[0]
    return pl.pallas_call(
        functools.partial(point_kernel, owners=owners),
        out_shape=[piece(width)] * 2 + [piece(blocks // 2 - width)] * 2 + [mode_sum] * 2,
        in_specs=[smem] * 3 + [anywhere] * 5 + [vmem] * 4,
        out_specs=[anywhere] * 6,
        scratch_shapes=[
            pltpu.VMEM((2, blocks + 1, rows, LANES), jnp.float32),
            pltpu.VMEM((blocks + 1, 2, rows, LANES), jnp.float32),
            pltpu.VMEM((2, side, 2 * side), jnp.float32),
            *[pltpu.VMEM((2, side, side), jnp.float32)] * 2,
            *[pltpu.VMEM((2 * side, 2 * side), jnp.bfloat16)] * 4,
            *[pltpu.VMEM((2 * side, 2 * side), jnp.float32)] * 2,
            pltpu.SemaphoreType.DMA((6 * blocks,)),
            pltpu.SemaphoreType.DMA((owners + 2,)),
        ],
        compiler_params=pltpu.CompilerParams(vmem_limit_bytes=24 * 1024 * 1024),
        cost_estimate=pl.CostEstimate(
            flops=slots * 32 * 2 * side**3, bytes_accessed=16 * 1024 * 1024, transcendentals=0
        ),
        name="point_sums",
    )(place, counts, spots, own, *halos, *prepared)


def with_neighbours(first, second, turns=(0, 1)):
    count = lax.axis_size("tiles")
    pairs = [(i, i + 1) for i in range(count - 1)]
    return [
        lax.ppermute(cells, "tiles", [x for a, b in pairs[turn::2] for x in ((a, b), (b, a))])
        for turn, cells in zip(turns, (first, second))
    ]


def swap(cells):
    return lax.ppermute(cells, "modes", [(0, 1), (1, 0)])


def rotated(cells, axis, step):
    count = lax.axis_size(axis)
    return lax.ppermute(cells, axis, [(i, (i + step) % count) for i in range(count)])


def small_kernel(body, out_shape, *args, name):
    return pl.pallas_call(
        body,
        out_shape=out_shape,
        in_specs=[
            pl.BlockSpec(memory_space=pltpu.SMEM if x.dtype == jnp.int32 else pltpu.VMEM)
            for x in args
        ],
        out_specs=jax.tree.map(lambda _: pl.BlockSpec(memory_space=pltpu.VMEM), out_shape),
        compiler_params=pltpu.CompilerParams(vmem_limit_bytes=4 * 1024 * 1024),
        cost_estimate=pl.CostEstimate(flops=0, bytes_accessed=0, transcendentals=0),
        name=name,
    )(*args)


def shape(*dims):
    return jax.ShapeDtypeStruct(dims, jnp.float32)


def after(cells, *earlier):
    return lax.optimization_barrier((cells, *earlier))[0]


def add_kernel(*refs):
    total = refs[0][...]
    for ref in refs[1:-1]:
        total = total + ref[...]
    refs[-1][...] = total


def others_kernel(kept, got, *outs):
    width, _, rows = outs[1].shape[:3]
    rim = outs[0].shape[2] // 2
    for step in range(len(outs) // 2):
        rims, core = outs[2 * step : 2 * step + 2]
        cut = slice(step * width, (step + 1) * width)
        rims[:, :, :rim] = kept[cut, :, :rim] + got[cut, :, :rim]
        rims[:, :, rim:] = kept[cut, :, rim + rows :] + got[cut, :, rim + rows :]
        core[...] = kept[cut, :, rim : rim + rows] + got[cut, :, rim : rim + rows]


def mine_kernel(place, kept, got, *rest):
    first, core, second = rest[-3:]
    rim, rows = first.shape[2], core.shape[2]
    total_above = kept[:, :, :rim] + got[:, :, :rim]
    total_below = kept[:, :, rim + rows :] + got[:, :, rim + rows :]
    for other in rest[:-3]:
        total_above = total_above + other[:, :, :rim]
        total_below = total_below + other[:, :, rim:]
    even = place[0] % 2 == 0

    @pl.when(even)
    def below_first():
        first[...] = total_below
        second[...] = total_above

    @pl.when(~even)
    def above_first():
        first[...] = total_above
        second[...] = total_below

    core[...] = kept[:, :, rim : rim + rows] + got[:, :, rim : rim + rows]


def fold_kernel(place, core, second, first, out):
    rim, rows = first.shape[2], core.shape[2]
    out[...] = core[...]
    near = pl.multiple_of((place[0] % 2) * (rows - rim), 8)
    far = pl.multiple_of(rows - rim - near, 8)
    out[:, :, pl.ds(far, rim)] += first[...]
    out[:, :, pl.ds(near, rim)] += second[...]


def finish_kernel(core, *rest):
    out = rest[-1]
    for block in range(core.shape[0]):
        total = core[block]
        for other in rest[:-1]:
            total = total + other[block]
        out[:, :, block * LANES : (block + 1) * LANES] = total


def share_rows(index, share):
    return pl.ds(pl.multiple_of(index * share, share), share)


def shares_kernel(place, kept, got, *outs):
    share = outs[0].shape[0]
    for step, out in enumerate(outs):
        rows = share_rows(place[0] ^ step, share)
        out[...] = kept[rows] + got[rows]


def end_kernel(place, *refs, others, tiles):
    folded, *core_in = refs[: 1 + others]
    parts = refs[1 + others : 1 + others + 2 * tiles]
    object_out, probe_out, whole, sems = refs[1 + others + 2 * tiles :]
    share = parts[0].shape[0]
    copies = []
    for index, part in enumerate(parts):
        swapped, step = divmod(index, tiles)
        mode = place[2] if swapped == 0 else 1 - place[2]
        target = probe_out.at[mode, share_rows(place[0] ^ step, share)]
        copies.append(pltpu.make_async_copy(part, target, sems.at[index]))
    for copy in copies:
        copy.start()
    finish_kernel(folded, *core_in, whole)
    copies.append(pltpu.make_async_copy(whole, object_out, sems.at[len(parts)]))
    copies[-1].start()
    for copy in copies:
        copy.wait()


def end_sums(place, folded, core_in, parts):
    width, planes, rows, lanes = folded.shape
    share, probe_cols = parts[0].shape
    tiles = len(parts) // 2
    grad = (planes, rows, width * lanes)
    args = [folded, *core_in, *parts]
    return pl.pallas_call(
        functools.partial(end_kernel, others=len(core_in), tiles=tiles),
        out_shape=[shape(*grad), shape(2, tiles * share, probe_cols)],
        in_specs=[pl.BlockSpec(memory_space=pltpu.SMEM)]
        + [pl.BlockSpec(memory_space=pltpu.VMEM)] * len(args),
        out_specs=[pl.BlockSpec(memory_space=pl.ANY)] * 2,
        scratch_shapes=[
            pltpu.VMEM(grad, jnp.float32),
            pltpu.SemaphoreType.DMA((len(parts) + 1,)),
        ],
        compiler_params=pltpu.CompilerParams(vmem_limit_bytes=4 * 1024 * 1024),
        name="end_sums",
    )(place, *args)


def gather_kernel(place, *refs):
    out, sems = refs[-2:]
    parts = refs[:-2]
    tiles = len(parts) // 2
    share = parts[0].shape[0]
    copies = []
    for index, part in enumerate(parts):
        swapped, step = divmod(index, tiles)
        mode = place[2] if swapped == 0 else 1 - place[2]
        target = out.at[mode, share_rows(place[0] ^ step, share)]
        copies.append(pltpu.make_async_copy(part, target, sems.at[index]))
    for copy in copies:
        copy.start()
    for copy in copies:
        copy.wait()


def gather_parts(place, parts):
    tiles = len(parts) // 2
    share, width = parts[0].shape
    return pl.pallas_call(
        gather_kernel,
        out_shape=shape(2, tiles * share, width),
        in_specs=[pl.BlockSpec(memory_space=pltpu.SMEM)]
        + [pl.BlockSpec(memory_space=pltpu.VMEM)] * len(parts),
        out_specs=pl.BlockSpec(memory_space=pl.ANY),
        scratch_shapes=[pltpu.SemaphoreType.DMA((len(parts),))],
        compiler_params=pltpu.CompilerParams(vmem_limit_bytes=4 * 1024 * 1024),
        name="probe_gather",
    )(place, *parts)


def on_device(object_field, probe, intensity, centres, counts):
    side = probe.shape[1]
    rim = side // 2
    strip_rows, cols = object_field.shape[1:]
    strip = lax.axis_index("tiles")
    sub = lax.axis_index("sub")
    mode = lax.axis_index("modes")
    tiles, subs = lax.axis_size("tiles"), lax.axis_size("sub")
    owners = subs * lax.axis_size("modes")
    width = cols // owners // LANES
    place = jnp.stack([strip, sub, mode]).astype(jnp.int32)

    last = strip_rows - rim
    even = strip % 2 == 0
    ends = [
        lax.dynamic_slice(object_field, (mode, jnp.where(at_end, last, 0), 0), (1, rim, cols))[0]
        for at_end in (even, ~even)
    ]
    first, second = with_neighbours(*ends)
    halos = (first, second, swap(first), swap(second))

    keep_mine, give_mine, keep_others, give_others, keep_probe, give_probe = point_sums(
        place, counts, centres.reshape(-1), object_field, halos, prepare(probe, intensity[0]), owners
    )
    got_probe = swap(give_probe)
    got_others = swap(give_others)
    got_mine = swap(give_mine)

    rims_shape = shape(width, 2, 2 * rim, LANES)
    core_shape = shape(width, 2, strip_rows, LANES)
    direct = tiles in (1, 2, 4)
    total_rows, total_cols = keep_probe.shape
    share = shape(total_rows // tiles, total_cols)
    if direct:
        parts = small_kernel(
            shares_kernel, [share] * tiles, place, keep_probe, got_probe, name="probe_shares"
        )
        got_others, *parts = lax.optimization_barrier((got_others, *parts))
    outgoing = list(small_kernel(
        others_kernel,
        [rims_shape, core_shape] * (subs - 1),
        keep_others,
        got_others,
        name="object_others",
    ))

    def rotate_all(parts):
        return [rotated(x, "sub", step + 1) for step, x in enumerate(parts)]

    def rotate_strips(parts):
        return [
            lax.ppermute(x, "tiles", [(i, i ^ (step + 1)) for i in range(tiles)])
            for step, x in enumerate(parts)
        ]

    if direct:
        parts_in = rotate_strips(parts[1:])
    rims_in = rotate_all(outgoing[0::2])
    core_out = outgoing[1::2]
    first, core, second = small_kernel(
        mine_kernel,
        [shape(width, 2, rim, LANES), core_shape, shape(width, 2, rim, LANES)],
        place,
        keep_mine,
        got_mine,
        *rims_in,
        name="object_mine",
    )
    if direct:
        part_sum = small_kernel(add_kernel, share, parts[0], *parts_in, name="probe_strips_sum")
        part_sum, first, second = lax.optimization_barrier((part_sum, first, second))
        part_in = [rotated(part_sum, "sub", step) for step in range(1, subs)]
    second, first = with_neighbours(second, first, (1, 0))
    if direct:
        part_sum = small_kernel(add_kernel, share, part_sum, *part_in, name="probe_total")
        part_sum, core, *core_out = lax.optimization_barrier((part_sum, core, *core_out))
        parts_in = rotate_strips([part_sum] * (tiles - 1))
    folded = small_kernel(
        fold_kernel, core_shape, place, core, second, first, name="object_fold"
    )
    if direct:
        parts_in[1], folded = lax.optimization_barrier((parts_in[1], folded))
    core_in = rotate_all(core_out)
    if direct:
        parts = [part_sum, *parts_in]
        return tuple(end_sums(place, folded, core_in, [*parts, *[swap(x) for x in parts]]))
    object_grad = small_kernel(
        finish_kernel,
        shape(2, strip_rows, width * LANES),
        folded,
        *core_in,
        name="object_finish",
    )
    parts = [lax.psum(keep_probe + got_probe, ("tiles", "sub"))]
    spot = place * jnp.array([0, 0, 1], jnp.int32)
    probe_grad = gather_parts(spot, [*parts, *[swap(x) for x in parts]])
    return (object_grad, probe_grad)


def solution(mesh):
    return jax.shard_map(
        on_device,
        mesh=mesh,
        in_specs=(
            P(None, ("groups", "tiles"), None),
            P("groups", None, None),
            P(("groups", "tiles"), ("sub", "modes"), None, None),
            P(("groups", "tiles"), None, None),
            P(("groups", "tiles")),
        ),
        out_specs=(P(None, ("groups", "tiles"), ("sub", "modes")), P("groups", None, None)),
        check_vma=False,
    )
```
